32 devices in a mesh: gx: 8 (over z, core), gy: 4 (over y, x).
Axes of the slice: x: 2, y: 2, z: 4, core: 2. Of those that a mesh axis runs over, the one named last changes fastest.
Arguments:
- atom_cell: int32 [3, 8, 8, 128, 576], P(None, 'gx', 'gy'), may hold values from 0 to 7
- atom_frac: float32 [3, 8, 8, 128, 576], P(None, 'gx', 'gy'), may hold values from 0 to 1
- atom_weight: float32 [8, 8, 128, 576], P('gx', 'gy'), may hold values from 0.5 to 1.5
- block_count: int32 [8, 8, 128], P('gx', 'gy'), may hold values from 384 to 576, as said below
- miller_h: int32 [8], replicated, may hold values from 9 to 12
- miller_k: int32 [8], replicated, may hold values from 9 to 12
- miller_l: int32 [8], replicated, may hold values from 9 to 204
Outputs:
- density: float32 [64, 64, 1024], P('gx', 'gy')
- intensity: float32 [128, 256], P(('gx', 'gy'))
The draws below stay inside these ranges and needn't reach their ends.
Inputs may be any that keep to these rules, and one draw needn't show every extreme that they name: `block_count`: slots 0 to count - 1 of a block hold its atoms; every device holds a block with exactly 576 atoms.
All inputs are finite; a program needn't handle non-finite values.
Results may differ from the reference program's by a relative error of at most 0.0023.
Values sent between devices are 32-bit elements; how exact they have to be, the bound alone decides.
No kernel may reach another device: no remote copies, remote signals or barrier semaphores. Data moves between devices by JAX's collectives and lax.ppermute only.
A program may use at most 192 MiB of HBM per device.

```python
import math
import jax
import jax.numpy as jnp
from jax import lax

CX = 8
CY = 16
CZ = 1024
CAP = 576
WINDOWS = 8
NX = 64
NY = 64


def draw_block_count(key, part):
    extent = (NX // 8, NY // 8, CZ // 8)
    counts = jax.random.randint(key, extent, CAP * 2 // 3, CAP + 1, dtype=jnp.int32)
    per_x = CX // 8
    per_y = CY // 8
    chosen = jax.random.randint(jax.random.fold_in(key, 7), (NX // CX, NY // CY), 0, CZ // 8, dtype=jnp.int32)
    owner_x = jnp.arange(NX // 8, dtype=jnp.int32) // per_x
    owner_y = jnp.arange(NY // 8, dtype=jnp.int32) // per_y
    target = chosen[owner_x][:, owner_y]
    corner_block = (jnp.arange(NX // 8) % per_x == 0)[:, None] & (jnp.arange(NY // 8) % per_y == 0)[None, :]
    forced = corner_block[:, :, None] & (jnp.arange(CZ // 8, dtype=jnp.int32)[None, None, :] == target[:, :, None])
    return jnp.where(forced, jnp.full(extent, CAP, jnp.int32), counts)


def touch_ends(values, key, low, high):
    longest = values.shape.index(max(values.shape))
    spots = []
    for shift in (0, 1):
        where = [jax.random.randint(jax.random.fold_in(key, axis), (), 0, length) for axis, length in enumerate(values.shape)]
        where[longest] = (where[longest] + shift) % values.shape[longest]
        spots.append(tuple(where))
    return values.at[spots[0]].set(low).at[spots[1]].set(high)


def levels(stream_key, shape, split, least, largest):
    loudness = 1.0
    for dim, blocks in split:
        steps = jax.random.uniform(jax.random.fold_in(jax.random.fold_in(stream_key, 6), dim), (blocks,), jnp.float32, least / len(split), largest / len(split))
        loudness = loudness * jnp.repeat(jnp.exp(steps), shape[dim] // blocks).reshape((-1,) + (1,) * (len(shape) - 1 - dim))
    return loudness


def setup_inputs(seed: int = 0) -> dict:
    streams_of = jax.random.split(jax.random.key(seed), 8)
    atom_cell = touch_ends(jax.random.randint(streams_of[0], (3, NX // 8, NY // 8, CZ // 8, CAP), 0, 8), jax.random.fold_in(streams_of[0], 1), 0, 7).astype(jnp.int32)
    atom_frac = jnp.clip(1.0 * jax.random.uniform(streams_of[1], (3, NX // 8, NY // 8, CZ // 8, CAP), jnp.float32) ** levels(streams_of[1], (3, NX // 8, NY // 8, CZ // 8, CAP), ((1, 8), (2, 4)), -0.2, 0.2), 0.0, 1.0)
    atom_weight = jnp.clip(0.5 + 1.0 * jax.random.uniform(streams_of[2], (NX // 8, NY // 8, CZ // 8, CAP), jnp.float32) ** levels(streams_of[2], (NX // 8, NY // 8, CZ // 8, CAP), ((0, 8), (1, 4)), -0.2, 0.2), 0.5, 1.5)
    block_count = draw_block_count(jax.random.fold_in(streams_of[7], 71), 0)
    miller_h = touch_ends(jax.random.randint(streams_of[4], (WINDOWS,), 9, NX // 5 + 1), jax.random.fold_in(streams_of[4], 1), 9, (NX // 5 + 1) - 1).astype(jnp.int32)
    miller_k = touch_ends(jax.random.randint(streams_of[5], (WINDOWS,), 9, NY // 5 + 1), jax.random.fold_in(streams_of[5], 1), 9, (NY // 5 + 1) - 1).astype(jnp.int32)
    miller_l = touch_ends(jax.random.randint(streams_of[6], (WINDOWS,), 9, CZ // 5 + 1), jax.random.fold_in(streams_of[6], 1), 9, (CZ // 5 + 1) - 1).astype(jnp.int32)
    return dict(atom_cell=atom_cell, atom_frac=atom_frac, atom_weight=atom_weight, block_count=block_count, miller_h=miller_h, miller_k=miller_k, miller_l=miller_l)


KERNEL_SIGMA = 0.9
NORMAL = 1.0 / (KERNEL_SIGMA * math.sqrt(2.0 * math.pi))
EXACT_DOT = lax.Precision.HIGHEST

def kernel_taps(offsets, fraction):
    tap_rows = jnp.arange(16, dtype=jnp.int32)
    differ = tap_rows - offsets[..., None]
    inside = (differ >= 1) & (differ <= 8)
    distance = (differ - 4).astype(jnp.float32) - fraction[..., None]
    values = jnp.exp(distance * distance * (-0.5 / (KERNEL_SIGMA * KERNEL_SIGMA))) * NORMAL
    return jnp.where(inside, values, jnp.zeros_like(values))

def to_bfloat(values):
    return lax.optimization_barrier(values.astype(jnp.bfloat16)).astype(jnp.float32)

def footprints(offsets, fraction, weights, counts):
    blocks, capacity = weights.shape
    slot_ids = jnp.arange(capacity, dtype=jnp.int32)
    occupied = (slot_ids[None, :] < counts[:, None]).astype(jnp.float32)
    taps_x = kernel_taps(offsets[0], fraction[0])
    taps_y = kernel_taps(offsets[1], fraction[1])
    taps_z = kernel_taps(offsets[2], fraction[2])
    scaled = to_bfloat((weights * occupied)[..., None] * taps_z)
    crossed = to_bfloat((taps_x[..., :, None] * taps_y[..., None, :]).reshape(blocks, capacity, 256))
    return jnp.einsum('bpc,bpm->bcm', scaled, crossed, precision=EXACT_DOT)

def pad_along(values, along, leading, trailing):
    widths = [(0, 0)] * values.ndim
    widths[along] = (leading, trailing)
    return jnp.pad(values, widths)

def wrap_fold(padded, along, length):
    interior = lax.slice_in_dim(padded, 4, length + 4, axis=along)
    leading = lax.slice_in_dim(padded, 0, 4, axis=along)
    trailing = lax.slice_in_dim(padded, length + 4, length + 8, axis=along)
    return interior + pad_along(trailing, along, 0, length - 4) + pad_along(leading, along, length - 4, 0)

def z_column(foot, depth_cells):
    nblocks = foot.shape[0]
    halves = foot.reshape(nblocks, 2, 8, 256)
    lower_half = pad_along(halves[:, 0], 0, 0, 1)
    upper_half = pad_along(halves[:, 1], 0, 1, 0)
    joined = (lower_half + upper_half).reshape((nblocks + 1) * 8, 256)
    folded = wrap_fold(joined, 0, depth_cells)
    return jnp.transpose(folded, (1, 0)).reshape(16, 16, depth_cells)

def phases(freqs, positions, extent):
    shifted = freqs[:, None] + jnp.arange(16, dtype=jnp.int32)[None, :] - 8
    product = positions[:, None, None] * shifted[None, :, :] % extent
    angles = product.astype(jnp.float32) * (2.0 * math.pi / extent)
    return (jnp.cos(angles), jnp.sin(angles))

def reference(atom_cell, atom_frac, atom_weight, block_count, miller_h, miller_k, miller_l):
    blocks_x, blocks_y, blocks_z, capacity = atom_weight.shape
    columns_total = blocks_x * blocks_y
    offsets = atom_cell.reshape(3, columns_total, blocks_z, capacity)
    fraction = atom_frac.reshape(3, columns_total, blocks_z, capacity)
    weights = atom_weight.reshape(columns_total, blocks_z, capacity)
    counts = block_count.reshape(columns_total, blocks_z)

    def deposit(padded_grid, column_index):
        foot = footprints(offsets[:, column_index], fraction[:, column_index], weights[column_index], counts[column_index])
        column = z_column(foot, CZ)
        start_x = (column_index // blocks_y * 8).astype(jnp.int32)
        start_y = (column_index % blocks_y * 8).astype(jnp.int32)
        anchor = jnp.zeros((), jnp.int32)
        current = lax.dynamic_slice(padded_grid, (start_x, start_y, anchor), (16, 16, CZ))
        return (lax.dynamic_update_slice(padded_grid, current + column, (start_x, start_y, anchor)), None)
    empty_grid = jnp.zeros((NX + 8, NY + 8, CZ), jnp.float32)
    padded_grid = lax.scan(deposit, empty_grid, jnp.arange(columns_total, dtype=jnp.int32))[0]
    density = wrap_fold(wrap_fold(padded_grid, 0, NX), 1, NY)
    windows = miller_h.shape[0]
    cos_z, sin_z = phases(miller_l, jnp.arange(CZ, dtype=jnp.int32), CZ)
    table_z = jnp.concatenate([cos_z, -sin_z], axis=1).reshape(CZ, 2 * windows * 16)
    partial_value = jnp.dot(density.reshape(NX * NY, CZ), table_z, precision=EXACT_DOT, preferred_element_type=jnp.float32)
    partial_value = partial_value.reshape(NX, NY, 2, windows, 16)
    part_real = partial_value[:, :, 0]
    part_imag = partial_value[:, :, 1]
    cos_y, sin_y = phases(miller_k, jnp.arange(NY, dtype=jnp.int32), NY)
    half_real = jnp.einsum('xywl,ywk->wxkl', part_real, cos_y, precision=EXACT_DOT) + jnp.einsum('xywl,ywk->wxkl', part_imag, sin_y, precision=EXACT_DOT)
    half_imag = jnp.einsum('xywl,ywk->wxkl', part_imag, cos_y, precision=EXACT_DOT) - jnp.einsum('xywl,ywk->wxkl', part_real, sin_y, precision=EXACT_DOT)
    cos_x, sin_x = phases(miller_h, jnp.arange(NX, dtype=jnp.int32), NX)
    wave_real = jnp.einsum('xwh,wxkl->whkl', cos_x, half_real, precision=EXACT_DOT) + jnp.einsum('xwh,wxkl->whkl', sin_x, half_imag, precision=EXACT_DOT)
    wave_imag = jnp.einsum('xwh,wxkl->whkl', cos_x, half_imag, precision=EXACT_DOT) - jnp.einsum('xwh,wxkl->whkl', sin_x, half_real, precision=EXACT_DOT)
    intensity = (wave_real * wave_real + wave_imag * wave_imag) / float(NX * NY * CZ)
    return (density, intensity.reshape(windows * 16, 256))
```

```python
import functools
import math
import jax, jax.numpy as jnp
from jax import lax
from jax.experimental import pallas as pl
from jax.experimental.pallas import tpu as pltpu
from jax.sharding import PartitionSpec as P
KERNEL_SIGMA=0.9
NORMAL=1.0/(KERNEL_SIGMA*math.sqrt(2.0*math.pi))
NT=(((1,),(1,)),((),()))
SCALE=math.sqrt(0.5/math.log(2.0))/KERNEL_SIGMA
LOGN=math.log2(NORMAL)

def deposit_body(count_ref,cell_ref,frac_ref,weight_ref,grid_ref,rows_ref,tx_ref,cross_ref,line_ref,*,blocks_z,cap):
    column=pl.program_id(0); chunk=pl.program_id(1)
    depth=8*blocks_z
    @pl.when(chunk==0)
    def _():
        line_ref[...]=jnp.zeros_like(line_ref)
    two=2*cap
    def paired(v): return jnp.concatenate([v[0:8],v[8:16]],axis=1)
    for d in range(3):
        cell=cell_ref[d,0,0].astype(jnp.float32)
        rows_ref[2*d]=paired(cell)
        rows_ref[2*d+1]=paired((cell+frac_ref[d,0,0])*SCALE)
    row16=lax.broadcasted_iota(jnp.int32,(16,cap),0)
    counts=jnp.zeros((16,cap),jnp.int32)
    for r in range(16):
        counts=jnp.where(row16==r,count_ref[0,column,chunk*16+r],counts)
    slots=lax.broadcasted_iota(jnp.int32,(16,cap),1)
    rows_ref[6]=paired(jnp.where(slots<counts,weight_ref[0,0],0.0))
    r8=lax.broadcasted_iota(jnp.int32,(8,two),0).astype(jnp.float32)
    low=(r8-4.0)*SCALE; high=(r8+4.0)*SCALE
    def taps(d,i):
        inside=r8>rows_ref[2*d,i:i+1,:]
        dist=jnp.where(inside,low,high)-rows_ref[2*d+1,i:i+1,:]
        val=jnp.exp2(LOGN-dist*dist)
        return inside,val
    edge=cap//128*128
    lanes=lax.broadcasted_iota(jnp.int32,(16,128),1)+edge
    for i in range(8):
        slot=i%2
        mx,vx=taps(0,i);
        tx_ref[slot,0:8]=jnp.where(mx,vx,0.0); tx_ref[slot,8:16]=jnp.where(mx,0.0,vx)
        my,vy=taps(1,i)
        ty=jnp.concatenate([jnp.where(my,vy,0.0),jnp.where(my,0.0,vy)],axis=0)
        mz,vz=taps(2,i); vz=vz*rows_ref[6,i:i+1,:]
        z=jnp.concatenate([jnp.where(mz,vz,0.0),jnp.where(mz,0.0,vz)],axis=0)
        for a in range(16):
            cross_ref[slot,16*a:16*a+16,:]=(tx_ref[slot,a:a+1,:]*ty).astype(jnp.bfloat16)
        if cap%128:
            mid=z[:,edge:edge+128]
            nz=jnp.zeros((16,edge),jnp.float32)
            za=jnp.concatenate([z[:,:edge],jnp.where(lanes<cap,mid,0.0),nz],axis=1)
            zb=jnp.concatenate([nz,jnp.where(lanes<cap,0.0,mid),z[:,edge+128:]],axis=1)
        else:
            nz=jnp.zeros((16,cap),jnp.float32)
            za=jnp.concatenate([z[:,:cap],nz],axis=1); zb=jnp.concatenate([nz,z[:,cap:]],axis=1)
        lhs=jnp.concatenate([za,zb],axis=0).astype(jnp.bfloat16)
        out=lax.dot_general(lhs,cross_ref[slot],NT,preferred_element_type=jnp.float32)
        base=pl.multiple_of(chunk*128+8*i,8)
        line_ref[pl.ds(base,16),:]+=out[0:16]
        line_ref[pl.ds(base+64,16),:]+=out[16:32]
    @pl.when(chunk==pl.num_programs(1)-1)
    def _():
        line_ref[4:8,:]+=line_ref[depth+4:depth+8,:]
        line_ref[depth:depth+4,:]+=line_ref[0:4,:]
        for c in range(depth//128):
            part=jnp.transpose(line_ref[128*c+4:128*c+132,:]).reshape(16,16,128)
            @pl.when(column==0)
            def _():
                grid_ref[:,0:16,128*c:128*c+128]=part
                grid_ref[:,16:24,128*c:128*c+128]=jnp.zeros((16,8,128),jnp.float32)
            @pl.when(column==1)
            def _():
                grid_ref[:,8:24,128*c:128*c+128]+=part

def deposit(cell,frac,weight,count):
    _,bx,by,bz,cap=cell.shape
    body=functools.partial(deposit_body,blocks_z=bz,cap=cap)
    return pl.pallas_call(body,
        grid=(by,bz//16),
        in_specs=[pl.BlockSpec(memory_space=pltpu.SMEM),
                  pl.BlockSpec((3,1,1,16,cap),lambda j,c:(0,0,j,c,0)),
                  pl.BlockSpec((3,1,1,16,cap),lambda j,c:(0,0,j,c,0)),
                  pl.BlockSpec((1,1,16,cap),lambda j,c:(0,j,c,0))],
        out_specs=pl.BlockSpec((16,8*by+8,8*bz),lambda j,c:(0,0,0)),
        out_shape=jax.ShapeDtypeStruct((16,8*by+8,8*bz),jnp.float32),
        scratch_shapes=[pltpu.VMEM((7,8,2*cap),jnp.float32),pltpu.VMEM((2,16,2*cap),jnp.float32),
                        pltpu.VMEM((2,256,2*cap),jnp.bfloat16),pltpu.VMEM((8*bz+8,256),jnp.float32)],
        compiler_params=pltpu.CompilerParams(vmem_limit_bytes=40<<20),
    )(count,cell,frac,weight)


def turn(freqs, place, extent):
    product = freqs * place
    if extent & (extent - 1) == 0:
        product = product & (extent - 1)
    else:
        product = lax.rem(lax.rem(product, extent) + extent, extent)
    angle = product.astype(jnp.float32) * (2.0 * math.pi / extent)
    return jnp.cos(angle), jnp.sin(angle)


def times(one, other):
    return (
        one[0] * other[0] - one[1] * other[1],
        one[0] * other[1] + one[1] * other[0],
    )


def split(value):
    head = value.astype(jnp.bfloat16)
    return head, (value - head.astype(jnp.float32)).astype(jnp.bfloat16)


def amplitude_body(
    place_ref, h_ref, k_ref, l_ref, grid_ref, out_ref,
    phase_ref, shift_ref, along_z_ref, half_ref, wave_ref, *, total_x, total_y
):
    rows_x, rows_y, depth = grid_ref.shape
    windows = h_ref.shape[0]
    wide = 16 * windows

    def centres(ref, shape):
        window = lax.broadcasted_iota(jnp.int32, shape, 1) // 16
        found = jnp.zeros(shape, jnp.int32)
        for w in range(windows):
            found = jnp.where(window == w, ref[w], found)
        return found

    block = 32
    below = lax.broadcasted_iota(jnp.int32, (block, wide), 0)
    freq_l = centres(l_ref, (block, wide)) + lax.rem(lax.broadcasted_iota(jnp.int32, (block, wide), 1), 16) - 8
    fine = turn(freq_l, below, depth)
    coarse = turn(freq_l, below * block, depth)
    shift_ref[0] = coarse[0]
    shift_ref[1] = coarse[1]
    for step in range(depth // block):
        now = times(fine, (shift_ref[0, step : step + 1], shift_ref[1, step : step + 1]))
        at = pl.ds(step * block, block)
        phase_ref[at, 0:wide] = now[0]
        phase_ref[at, wide : 2 * wide] = -now[1]
    value, rest = split(grid_ref[...].reshape(rows_x * rows_y, depth))
    table, left = split(phase_ref[...])

    def dot(a, b):
        return jnp.dot(a, b, preferred_element_type=jnp.float32)

    along_z_ref[...] = (dot(value, table) + (dot(value, left) + dot(rest, table))).reshape(
        rows_x, rows_y, 2 * wide
    )
    row16 = lax.broadcasted_iota(jnp.int32, (16, wide), 0)
    freq_k = centres(k_ref, (16, wide)) + row16 - 8
    now = turn(freq_k, place_ref[1] + 2 * total_y, total_y)
    step = turn(freq_k, 1, total_y)
    for y in range(rows_y):
        phase_ref[pl.ds(32 * y, 16), 0:wide] = now[0]
        phase_ref[pl.ds(32 * y + 16, 16), 0:wide] = now[1]
        now = times(now, step)
    group = 4
    for x in range(0, rows_x, group):
        real = [jnp.zeros((16, wide), jnp.float32)] * group
        imag = [jnp.zeros((16, wide), jnp.float32)] * group
        for y in range(rows_y):
            cos = phase_ref[pl.ds(32 * y, 16), 0:wide]
            sin = phase_ref[pl.ds(32 * y + 16, 16), 0:wide]
            for g in range(group):
                a = along_z_ref[x + g, y : y + 1, 0:wide]
                b = along_z_ref[x + g, y : y + 1, wide : 2 * wide]
                real[g] = real[g] + (a * cos + b * sin)
                imag[g] = imag[g] + (b * cos - a * sin)
        for g in range(group):
            half_ref[x + g, 0:16] = real[g]
            half_ref[x + g, 16:32] = imag[g]
    freq_h = centres(h_ref, (16, wide)) + row16 - 8
    now = turn(freq_h, place_ref[0] + 2 * total_x, total_x)
    step = turn(freq_h, 1, total_x)
    for x in range(rows_x):
        phase_ref[pl.ds(32 * x, 16), wide : 2 * wide] = now[0]
        phase_ref[pl.ds(32 * x + 16, 16), wide : 2 * wide] = now[1]
        now = times(now, step)
    for h in range(0, 16, group):
        real = [jnp.zeros((16, wide), jnp.float32)] * group
        imag = [jnp.zeros((16, wide), jnp.float32)] * group
        for x in range(rows_x):
            a = half_ref[x, 0:16]
            b = half_ref[x, 16:32]
            for g in range(group):
                cos = phase_ref[32 * x + h + g : 32 * x + h + g + 1, wide : 2 * wide]
                sin = phase_ref[32 * x + 16 + h + g : 32 * x + 17 + h + g, wide : 2 * wide]
                real[g] = real[g] + (a * cos + b * sin)
                imag[g] = imag[g] + (b * cos - a * sin)
        for g in range(group):
            wave_ref[pl.ds(32 * (h + g), 16)] = real[g]
            wave_ref[pl.ds(32 * (h + g) + 16, 16)] = imag[g]
    turned = jnp.transpose(wave_ref[...])
    pieces, _, lanes = out_ref.shape
    per_window = pieces // windows
    for piece in range(pieces):
        w, part = piece // per_window, piece % per_window
        out_ref[piece] = turned[16 * w : 16 * w + 16, part * lanes : (part + 1) * lanes]


def amplitude(grid, place, miller_h, miller_k, miller_l, total_x, total_y, pieces):
    rows_x, rows_y, depth = grid.shape
    windows = miller_h.shape[0]
    wide = 16 * windows
    vmem = pl.BlockSpec(memory_space=pltpu.VMEM)
    smem = pl.BlockSpec(memory_space=pltpu.SMEM)
    return pl.pallas_call(
        functools.partial(amplitude_body, total_x=total_x, total_y=total_y),
        in_specs=[smem, smem, smem, smem, vmem],
        out_specs=vmem,
        out_shape=jax.ShapeDtypeStruct((pieces, 16, 32 * wide // pieces), jnp.float32),
        scratch_shapes=[
            pltpu.VMEM((max(depth, 32 * rows_y, 32 * rows_x), 2 * wide), jnp.float32),
            pltpu.VMEM((2, 32, wide), jnp.float32),
            pltpu.VMEM((rows_x, rows_y, 2 * wide), jnp.float32),
            pltpu.VMEM((rows_x, 32, wide), jnp.float32),
            pltpu.VMEM((512, wide), jnp.float32),
        ],
        compiler_params=pltpu.CompilerParams(vmem_limit_bytes=40 << 20),
    )(place, miller_h, miller_k, miller_l, grid)


def with_margins(cells, axis, dim):
    count = lax.axis_size(axis)
    length = cells.shape[dim] - 8
    head = lax.slice_in_dim(cells, 0, 4, axis=dim)
    tail = lax.slice_in_dim(cells, length + 4, length + 8, axis=dim)
    before = lax.ppermute(tail, axis, [(i, (i + 1) % count) for i in range(count)])
    after = lax.ppermute(head, axis, [((i + 1) % count, i) for i in range(count)])
    inner = lax.slice_in_dim(cells, 4, length + 4, axis=dim)
    parts = [lax.slice_in_dim(inner, 0, 4, axis=dim) + before]
    if length > 8:
        parts.append(lax.slice_in_dim(inner, 4, length - 4, axis=dim))
    parts.append(lax.slice_in_dim(inner, length - 4, length, axis=dim) + after)
    return jnp.concatenate(parts, axis=dim)


def shards(atom_cell, atom_frac, atom_weight, block_count, miller_h, miller_k, miller_l):
    blocks_x, blocks_y, blocks_z, _ = atom_weight.shape
    count_x, count_y = lax.axis_size("gx"), lax.axis_size("gy")
    width_x, width_y, depth = 8 * blocks_x, 8 * blocks_y, 8 * blocks_z
    total_x, total_y = width_x * count_x, width_y * count_y
    grid = deposit(atom_cell, atom_frac, atom_weight, block_count)
    place = jnp.stack([lax.axis_index("gx") * width_x - 4, lax.axis_index("gy") * width_y - 4])
    pieces = count_x * count_y
    waves = amplitude(
        grid, place.astype(jnp.int32), miller_h, miller_k, miller_l, total_x, total_y, pieces
    )
    waves = lax.all_to_all(waves, ("gx", "gy"), 0, 0, tiled=False)
    rows = miller_h.shape[0] * 16 // pieces
    summed = jnp.sum(waves, axis=0).reshape(16, rows, 2, 16)
    power = jnp.sum(summed * summed, axis=2) / float(total_x * total_y * depth)
    intensity = jnp.transpose(power, (1, 2, 0)).reshape(rows, 256)
    density = with_margins(with_margins(grid, "gx", 0), "gy", 1)
    return (density, intensity)


def solution(mesh):
    in_specs = (
        P(None, "gx", "gy", None, None),
        P(None, "gx", "gy", None, None),
        P("gx", "gy", None, None),
        P("gx", "gy", None),
        P(),
        P(),
        P(),
    )
    out_specs = (P("gx", "gy", None), P(("gx", "gy"), None))
    return jax.shard_map(shards, mesh=mesh, in_specs=in_specs, out_specs=out_specs, check_vma=False)
```

```python
import functools
import math
import jax, jax.numpy as jnp
from jax import lax
from jax.experimental import pallas as pl
from jax.experimental.pallas import tpu as pltpu
from jax.sharding import PartitionSpec as P
KERNEL_SIGMA=0.9
NORMAL=1.0/(KERNEL_SIGMA*math.sqrt(2.0*math.pi))
NT=(((1,),(1,)),((),()))
SCALE=math.sqrt(0.5/math.log(2.0))/KERNEL_SIGMA
LOGN=math.log2(NORMAL)
UNROLL=8
FAR=-1.0e4
def deposit_body(count_ref,cell_ref,frac_ref,weight_ref,head_ref,mid_ref,tail_ref,rows_ref,edge_ref,line_ref):
    column=pl.program_id(0)
    cap,blocks_z=cell_ref.shape[3:]
    depth=8*blocks_z; half=blocks_z//2; two=2*cap
    line_ref[...]=jnp.zeros_like(line_ref)
    def paired(v):
        v=jnp.transpose(v)
        return jnp.concatenate([v[0:half],v[half:]],axis=1).reshape(half//8,8,two)
    for d in range(3):
        cell=cell_ref[d,0,0].astype(jnp.float32)
        place=cell+frac_ref[d,0,0]
        if d==0:
            upper=jnp.where(cell>3.5,1.0,0.0)
            rows_ref[0]=paired((place-3.5)*SCALE)
            rows_ref[1]=paired(upper)
            rows_ref[2]=paired(cell-4.0*upper)
        else:
            rows_ref[2*d+1]=paired(place*SCALE)
            rows_ref[2*d+2]=paired(cell)
    slots=lax.broadcasted_iota(jnp.int32,(cap,blocks_z),0)
    rows_ref[7]=paired(jnp.where(slots<count_ref[0,pl.ds(column,1),:],weight_ref[0,0],0.0))
    row=lax.broadcasted_iota(jnp.int32,(8,128),0)
    r8=row.astype(jnp.float32)
    low=(r8-4.0)*SCALE; high=(r8+4.0)*SCALE
    r4=(row%4).astype(jnp.float32)
    second=row>=4
    nodes=(4.0*r4-6.0)*SCALE
    first=jnp.where(second,1.0,0.0)
    on0=jnp.where((r4>=first)&(r4<=first+1.0),0.0,FAR)
    on1=jnp.where((r4>=first+1.0)&(r4<=first+2.0),0.0,FAR)
    slopes=(r4-1.5)*(2.0*SCALE)
    sign=jnp.where(second,-1.0,1.0)
    bound=jnp.where(second,0.5-r4,r4)
    part=cap%128
    lanes=lax.broadcasted_iota(jnp.int32,(16,128),1)
    zero=jnp.zeros((16,128),jnp.float32)
    def group(g,carry):
        for u in range(UNROLL):
            slot=u%2
            i=g*UNROLL+u
            acc=[None,None]
            for t in range(two//128):
                def line(k): return rows_ref[k,g,u:u+1,128*t:128*t+128]
                rx=line(0)
                q=rx-nodes
                here=slot*(two//128)+t
                edge_ref[here,0:8]=jnp.exp2(jnp.where(line(1)>0.5,on1,on0)-q*q)
                edge_ref[here,8:16]=jnp.exp2(jnp.where(bound>sign*line(2),slopes*rx,FAR))
                def taps(d):
                    inside=r8>line(2*d+2)
                    dist=jnp.where(inside,low,high)-line(2*d+1)
                    return inside,jnp.exp2(LOGN-dist*dist)
                my,vy=taps(1)
                y=jnp.concatenate([jnp.where(my,vy,0.0),jnp.where(my,0.0,vy)],axis=0)
                mz,vz=taps(2); vz=vz*line(7)
                z=jnp.concatenate([jnp.where(mz,vz,0.0),jnp.where(mz,0.0,vz)],axis=0)
                def rows(values,first):
                    return jnp.concatenate([jnp.concatenate([(values*edge_ref[here,first+4*s+h:first+4*s+h+1,:]).astype(jnp.bfloat16) for h in range(4)],axis=0) for s in range(2)],axis=1)
                right=rows(y,8)
                if part and t==cap//128: sides=[(0,jnp.where(lanes<part,z,0.0)),(1,jnp.where(lanes<part,0.0,z))]
                else: sides=[(int(128*t>=cap),z)]
                for side,values in sides:
                    more=lax.dot_general(rows(values,0),right,NT,preferred_element_type=jnp.float32)
                    acc[side]=more if acc[side] is None else acc[side]+more
            base=pl.multiple_of(8*i,8)
            for s in range(2):
                for h in range(4):
                    line_ref[h,pl.ds(base+8*half*s,16),:]+=acc[s][16*h:16*h+16]
        return carry
    lax.fori_loop(0,half//UNROLL,group,0)
    outs=(head_ref,mid_ref,tail_ref)
    @pl.when(column==0)
    def _():
        for ref in outs: ref[...]=jnp.zeros_like(ref)
    for h in range(4):
        line_ref[h,4:8,:]+=line_ref[h,depth+4:depth+8,:]
        line_ref[h,depth:depth+4,:]+=line_ref[h,0:4,:]
    at=pl.ds(pl.multiple_of(8*column,8),16)
    for h in range(4):
        for c in range(depth//128):
            turned=jnp.transpose(line_ref[h,128*c+4:128*c+132,:])
            for k in range(4):
                near=k-1.5
                factor=NORMAL*math.exp((-near*(4*h-6)-0.5*near*near)/KERNEL_SIGMA**2)
                ref=outs[(h+1)//2]
                place=k if h!=2 else 4+k
                ref[place,at,128*c:128*c+128]+=turned[16*k:16*k+16]*factor

def deposit(cell,frac,weight,count):
    _,bx,by,bz,cap=cell.shape
    span=-(-cap//128)*128
    swap=lambda v: jnp.swapaxes(v,-1,-2)
    return pl.pallas_call(deposit_body,
        grid=(by,),
        in_specs=[pl.BlockSpec((1,by,bz),lambda j:(0,0,0)),
                  pl.BlockSpec((3,1,1,cap,bz),lambda j:(0,0,j,0,0)),
                  pl.BlockSpec((3,1,1,cap,bz),lambda j:(0,0,j,0,0)),
                  pl.BlockSpec((1,1,cap,bz),lambda j:(0,j,0,0))],
        out_specs=[pl.BlockSpec((n,8*by+8,8*bz),lambda j:(0,0,0)) for n in (4,8,4)],
        out_shape=[jax.ShapeDtypeStruct((n,8*by+8,8*bz),jnp.float32) for n in (4,8,4)],
        scratch_shapes=[pltpu.VMEM((8,bz//16,8,2*cap),jnp.float32),pltpu.VMEM((2*(2*cap//128),16,128),jnp.float32),
                        pltpu.VMEM((4,8*bz+8,64),jnp.float32)],
        compiler_params=pltpu.CompilerParams(vmem_limit_bytes=62<<20),
    )(count,swap(cell),swap(frac),swap(weight))


def turn(freqs, place, extent):
    product = freqs * place
    if extent & (extent - 1) == 0:
        product = product & (extent - 1)
    else:
        product = lax.rem(lax.rem(product, extent) + extent, extent)
    angle = product.astype(jnp.float32) * (2.0 * math.pi / extent)
    return jnp.cos(angle), jnp.sin(angle)


def times(one, other):
    return (
        one[0] * other[0] - one[1] * other[1],
        one[0] * other[1] + one[1] * other[0],
    )


def split(value):
    head = value.astype(jnp.bfloat16)
    return head, (value - head.astype(jnp.float32)).astype(jnp.bfloat16)


def amplitude_body(
    place_ref, h_ref, k_ref, l_ref, head_ref, mid_ref, tail_ref, out_ref,
    phase_ref, shift_ref, along_z_ref, half_ref, wave_ref, *, total_x, total_y
):
    rows_x, rows_y, _ = along_z_ref.shape
    depth = mid_ref.shape[2]
    windows = h_ref.shape[0]
    wide = 16 * windows

    def centres(ref, shape):
        window = lax.broadcasted_iota(jnp.int32, shape, 1) // 16
        found = jnp.zeros(shape, jnp.int32)
        for w in range(windows):
            found = jnp.where(window == w, ref[w], found)
        return found

    block = 32
    below = lax.broadcasted_iota(jnp.int32, (block, wide), 0)
    freq_l = centres(l_ref, (block, wide)) + lax.rem(lax.broadcasted_iota(jnp.int32, (block, wide), 1), 16) - 8
    fine = turn(freq_l, below, depth)
    coarse = turn(freq_l, below * block, depth)
    shift_ref[0] = coarse[0]
    shift_ref[1] = coarse[1]
    for step in range(depth // block):
        now = times(fine, (shift_ref[0, step : step + 1], shift_ref[1, step : step + 1]))
        at = pl.ds(step * block, block)
        phase_ref[at, 0:wide] = now[0]
        phase_ref[at, wide : 2 * wide] = -now[1]
    table, left = split(phase_ref[0:depth])

    def dot(a, b):
        return jnp.dot(a, b, preferred_element_type=jnp.float32)

    start = 0
    for ref in (head_ref, mid_ref, tail_ref):
        count = ref.shape[0]
        value, rest = split(ref[...].reshape(count * rows_y, depth))
        found = dot(value, table) + (dot(value, left) + dot(rest, table))
        along_z_ref[start : start + count] = found.reshape(count, rows_y, 2 * wide)
        start += count
    row16 = lax.broadcasted_iota(jnp.int32, (16, wide), 0)
    freq_k = centres(k_ref, (16, wide)) + row16 - 8
    now = turn(freq_k, place_ref[1] + 2 * total_y, total_y)
    step = turn(freq_k, 1, total_y)
    for y in range(rows_y):
        phase_ref[pl.ds(32 * y, 16), 0:wide] = now[0]
        phase_ref[pl.ds(32 * y + 16, 16), 0:wide] = now[1]
        now = times(now, step)
    group = 4
    for x in range(0, rows_x, group):
        real = [jnp.zeros((16, wide), jnp.float32)] * group
        imag = [jnp.zeros((16, wide), jnp.float32)] * group
        for y in range(rows_y):
            cos = phase_ref[pl.ds(32 * y, 16), 0:wide]
            sin = phase_ref[pl.ds(32 * y + 16, 16), 0:wide]
            for g in range(group):
                a = along_z_ref[x + g, y : y + 1, 0:wide]
                b = along_z_ref[x + g, y : y + 1, wide : 2 * wide]
                real[g] = real[g] + (a * cos + b * sin)
                imag[g] = imag[g] + (b * cos - a * sin)
        for g in range(group):
            half_ref[x + g, 0:16] = real[g]
            half_ref[x + g, 16:32] = imag[g]
    freq_h = centres(h_ref, (16, wide)) + row16 - 8
    now = turn(freq_h, place_ref[0] + 2 * total_x, total_x)
    step = turn(freq_h, 1, total_x)
    for x in range(rows_x):
        phase_ref[pl.ds(32 * x, 16), wide : 2 * wide] = now[0]
        phase_ref[pl.ds(32 * x + 16, 16), wide : 2 * wide] = now[1]
        now = times(now, step)
    for h in range(0, 16, group):
        real = [jnp.zeros((16, wide), jnp.float32)] * group
        imag = [jnp.zeros((16, wide), jnp.float32)] * group
        for x in range(rows_x):
            a = half_ref[x, 0:16]
            b = half_ref[x, 16:32]
            for g in range(group):
                cos = phase_ref[32 * x + h + g : 32 * x + h + g + 1, wide : 2 * wide]
                sin = phase_ref[32 * x + 16 + h + g : 32 * x + 17 + h + g, wide : 2 * wide]
                real[g] = real[g] + (a * cos + b * sin)
                imag[g] = imag[g] + (b * cos - a * sin)
        for g in range(group):
            wave_ref[pl.ds(32 * (h + g), 16)] = real[g]
            wave_ref[pl.ds(32 * (h + g) + 16, 16)] = imag[g]
    turned = jnp.transpose(wave_ref[...])
    pieces, _, lanes = out_ref.shape
    per_window = pieces // windows
    for piece in range(pieces):
        w, part = piece // per_window, piece % per_window
        out_ref[piece] = turned[16 * w : 16 * w + 16, part * lanes : (part + 1) * lanes]


def amplitude(grids, place, miller_h, miller_k, miller_l, total_x, total_y, pieces):
    _, rows_y, depth = grids[0].shape
    rows_x = sum(grid.shape[0] for grid in grids)
    windows = miller_h.shape[0]
    wide = 16 * windows
    vmem = pl.BlockSpec(memory_space=pltpu.VMEM)
    smem = pl.BlockSpec(memory_space=pltpu.SMEM)
    return pl.pallas_call(
        functools.partial(amplitude_body, total_x=total_x, total_y=total_y),
        in_specs=[smem, smem, smem, smem, vmem, vmem, vmem],
        out_specs=vmem,
        out_shape=jax.ShapeDtypeStruct((pieces, 16, 32 * wide // pieces), jnp.float32),
        scratch_shapes=[
            pltpu.VMEM((max(depth, 32 * rows_y, 32 * rows_x), 2 * wide), jnp.float32),
            pltpu.VMEM((2, 32, wide), jnp.float32),
            pltpu.VMEM((rows_x, rows_y, 2 * wide), jnp.float32),
            pltpu.VMEM((rows_x, 32, wide), jnp.float32),
            pltpu.VMEM((512, wide), jnp.float32),
        ],
        compiler_params=pltpu.CompilerParams(vmem_limit_bytes=40 << 20),
        cost_estimate=pl.CostEstimate(flops=5_000_000_000, bytes_accessed=8_000_000, transcendentals=100_000),
    )(place, miller_h, miller_k, miller_l, *grids)


def exchange(head, tail, axis):
    count = lax.axis_size(axis)
    before = lax.ppermute(tail, axis, [(i, (i + 1) % count) for i in range(count)])
    after = lax.ppermute(head, axis, [((i + 1) % count, i) for i in range(count)])
    return before, after


def added(inner, before, after, dim):
    length = inner.shape[dim]
    widths = [(0, 0)] * inner.ndim
    widths[dim] = (0, length - 4)
    leading = jnp.pad(before, widths)
    widths[dim] = (length - 4, 0)
    return inner + leading + jnp.pad(after, widths)


def shards(atom_cell, atom_frac, atom_weight, block_count, miller_h, miller_k, miller_l):
    blocks_x, blocks_y, blocks_z, _ = atom_weight.shape
    count_x, count_y = lax.axis_size("gx"), lax.axis_size("gy")
    width_x, width_y, depth = 8 * blocks_x, 8 * blocks_y, 8 * blocks_z
    total_x, total_y = width_x * count_x, width_y * count_y
    place = jnp.stack([lax.axis_index("gx") * width_x - 4, lax.axis_index("gy") * width_y - 4])
    grids = deposit(atom_cell, atom_frac, atom_weight, block_count)
    head, mid, tail = grids
    before, after = exchange(head, tail, "gx")
    pieces = count_x * count_y
    waves = amplitude(
        grids, place.astype(jnp.int32), miller_h, miller_k, miller_l, total_x, total_y, pieces
    )
    before, after, _ = lax.optimization_barrier((before, after, waves))
    received = lax.all_to_all(waves, ("gx", "gy"), 0, 0, tiled=False)
    rows = miller_h.shape[0] * 16 // pieces
    summed = jnp.sum(received, axis=0).reshape(16, rows, 2, 16)
    power = jnp.sum(summed * summed, axis=2) / float(total_x * total_y * depth)
    intensity = jnp.transpose(power, (1, 2, 0)).reshape(rows, 256)
    wide = added(mid, before, after, 0)
    before, after = exchange(wide[:, :4], wide[:, width_y + 4 :], "gy")
    density = added(wide[:, 4 : width_y + 4], before, after, 1)
    return (density, intensity)


def solution(mesh):
    in_specs = (
        P(None, "gx", "gy", None, None),
        P(None, "gx", "gy", None, None),
        P("gx", "gy", None, None),
        P("gx", "gy", None),
        P(),
        P(),
        P(),
    )
    out_specs = (P("gx", "gy", None), P(("gx", "gy"), None))
    return jax.shard_map(shards, mesh=mesh, in_specs=in_specs, out_specs=out_specs, check_vma=False)
```

```python
import functools
import math
import jax, jax.numpy as jnp
from jax import lax
from jax.experimental import pallas as pl
from jax.experimental.pallas import tpu as pltpu
from jax.sharding import PartitionSpec as P
KERNEL_SIGMA=0.9
NORMAL=1.0/(KERNEL_SIGMA*math.sqrt(2.0*math.pi))
NT=(((1,),(1,)),((),()))
SCALE=math.sqrt(0.5/math.log(2.0))/KERNEL_SIGMA
LOGN=math.log2(NORMAL)
UNROLL=8
FAR=-1.0e4
def deposit_body(count_ref,cell_ref,frac_ref,weight_ref,head_ref,mid_ref,tail_ref,rows_ref,edge_ref,line_ref):
    column=pl.program_id(0)
    cap,blocks_z=cell_ref.shape[3:]
    depth=8*blocks_z; half=blocks_z//2; two=2*cap
    line_ref[...]=jnp.zeros_like(line_ref)
    def paired(v):
        v=jnp.transpose(v)
        return jnp.concatenate([v[0:half],v[half:]],axis=1).reshape(half//8,8,two)
    for d in range(3):
        cell=cell_ref[d,0,0].astype(jnp.float32)
        place=cell+frac_ref[d,0,0]
        if d==0:
            upper=jnp.where(cell>3.5,1.0,0.0)
            rows_ref[0]=paired((place-3.5)*SCALE)
            rows_ref[1]=paired(upper)
            rows_ref[2]=paired(cell-4.0*upper)
        else:
            rows_ref[2*d+1]=paired(place*SCALE)
            rows_ref[2*d+2]=paired(cell)
    slots=lax.broadcasted_iota(jnp.int32,(cap,blocks_z),0)
    rows_ref[7]=paired(jnp.where(slots<count_ref[0,pl.ds(column,1),:],weight_ref[0,0],0.0))
    row=lax.broadcasted_iota(jnp.int32,(8,128),0)
    r8=row.astype(jnp.float32)
    low=(r8-4.0)*SCALE; high=(r8+4.0)*SCALE
    r4=(row%4).astype(jnp.float32)
    second=row>=4
    nodes=(4.0*r4-6.0)*SCALE
    first=jnp.where(second,1.0,0.0)
    on0=jnp.where((r4>=first)&(r4<=first+1.0),0.0,FAR)
    on1=jnp.where((r4>=first+1.0)&(r4<=first+2.0),0.0,FAR)
    slopes=(r4-1.5)*(2.0*SCALE)
    sign=jnp.where(second,-1.0,1.0)
    bound=jnp.where(second,0.5-r4,r4)
    part=cap%128
    lanes=lax.broadcasted_iota(jnp.int32,(16,128),1)
    none=jnp.zeros((16,128),jnp.bfloat16)
    def group(g,carry):
        for u in range(UNROLL):
            slot=u%2
            i=g*UNROLL+u
            lefts=[[],[]]; rights=[[],[]]
            for t in range(two//128):
                def line(k): return rows_ref[k,g,u:u+1,128*t:128*t+128]
                rx=line(0)
                q=rx-nodes
                here=slot*(two//128)+t
                edge_ref[here,0:8]=jnp.exp2(jnp.where(line(1)>0.5,on1,on0)-q*q)
                edge_ref[here,8:16]=jnp.exp2(jnp.where(bound>sign*line(2),slopes*rx,FAR))
                def taps(d):
                    inside=r8>line(2*d+2)
                    dist=jnp.where(inside,low,high)-line(2*d+1)
                    return inside,jnp.exp2(LOGN-dist*dist)
                my,vy=taps(1)
                y=jnp.concatenate([jnp.where(my,vy,0.0),jnp.where(my,0.0,vy)],axis=0)
                mz,vz=taps(2); vz=vz*line(7)
                z=jnp.concatenate([jnp.where(mz,vz,0.0),jnp.where(mz,0.0,vz)],axis=0)
                def rows(values,first,dead):
                    sides=[]
                    for s in range(2):
                        sides.append(jnp.concatenate([none if (s,h) in dead else (values*edge_ref[here,first+4*s+h:first+4*s+h+1,:]).astype(jnp.bfloat16) for h in range(4)],axis=0))
                    return jnp.concatenate(sides,axis=1)
                right=rows(y,8,[(0,0)])
                if part and t==cap//128: sides=[(0,jnp.where(lanes<part,z,0.0)),(1,jnp.where(lanes<part,0.0,z))]
                else: sides=[(int(128*t>=cap),z)]
                for side,values in sides:
                    lefts[side].append(rows(values,0,[(0,3),(1,0)])); rights[side].append(right)
            base=pl.multiple_of(8*i,8)
            acc=[lax.dot_general(jnp.concatenate(l,axis=1),jnp.concatenate(r,axis=1),NT,preferred_element_type=jnp.float32) for l,r in zip(lefts,rights)]
            for s in range(2):
                for h in range(4):
                    line_ref[h,pl.ds(base+8*half*s,16),:]+=acc[s][16*h:16*h+16]
        return carry
    lax.fori_loop(0,half//UNROLL,group,0)
    outs=(head_ref,mid_ref,tail_ref)
    @pl.when(column==0)
    def _():
        for ref in outs: ref[...]=jnp.zeros_like(ref)
    for h in range(4):
        line_ref[h,4:8,:]+=line_ref[h,depth+4:depth+8,:]
        line_ref[h,depth:depth+4,:]+=line_ref[h,0:4,:]
    at=pl.ds(pl.multiple_of(8*column,8),16)
    for h in range(4):
        for c in range(depth//128):
            turned=jnp.transpose(line_ref[h,128*c+4:128*c+132,:])
            for k in range(4):
                near=k-1.5
                factor=NORMAL*math.exp((-near*(4*h-6)-0.5*near*near)/KERNEL_SIGMA**2)
                ref=outs[(h+1)//2]
                place=k if h!=2 else 4+k
                ref[place,at,128*c:128*c+128]+=turned[16*k:16*k+16]*factor

def deposit(cell,frac,weight,count):
    _,bx,by,bz,cap=cell.shape
    span=-(-cap//128)*128
    swap=lambda v: jnp.swapaxes(v,-1,-2)
    return pl.pallas_call(deposit_body,
        grid=(by,),
        in_specs=[pl.BlockSpec((1,by,bz),lambda j:(0,0,0)),
                  pl.BlockSpec((3,1,1,cap,bz),lambda j:(0,0,j,0,0)),
                  pl.BlockSpec((3,1,1,cap,bz),lambda j:(0,0,j,0,0)),
                  pl.BlockSpec((1,1,cap,bz),lambda j:(0,j,0,0))],
        out_specs=[pl.BlockSpec((n,8*by+8,8*bz),lambda j:(0,0,0)) for n in (4,8,4)],
        out_shape=[jax.ShapeDtypeStruct((n,8*by+8,8*bz),jnp.float32) for n in (4,8,4)],
        scratch_shapes=[pltpu.VMEM((8,bz//16,8,2*cap),jnp.float32),pltpu.VMEM((2*(2*cap//128),16,128),jnp.float32),
                        pltpu.VMEM((4,8*bz+8,64),jnp.float32)],
        compiler_params=pltpu.CompilerParams(vmem_limit_bytes=62<<20),
    )(count,swap(cell),swap(frac),swap(weight))


def turn(freqs, place, extent):
    product = freqs * place
    if extent & (extent - 1) == 0:
        product = product & (extent - 1)
    else:
        product = lax.rem(lax.rem(product, extent) + extent, extent)
    angle = product.astype(jnp.float32) * (2.0 * math.pi / extent)
    return jnp.cos(angle), jnp.sin(angle)


def times(one, other):
    return (
        one[0] * other[0] - one[1] * other[1],
        one[0] * other[1] + one[1] * other[0],
    )


def split(value):
    head = value.astype(jnp.bfloat16)
    return head, (value - head.astype(jnp.float32)).astype(jnp.bfloat16)


def amplitude_body(
    place_ref, h_ref, k_ref, l_ref, head_ref, mid_ref, tail_ref, out_ref,
    phase_ref, shift_ref, along_z_ref, half_ref, wave_ref, grid_ref, sems, *, total_x, total_y
):
    rows_x, rows_y, _ = along_z_ref.shape
    depth = mid_ref.shape[2]
    copies = []
    start = 0
    for n, ref in enumerate((head_ref, mid_ref, tail_ref)):
        target = grid_ref.at[pl.ds(start, ref.shape[0])]
        copies.append(pltpu.make_async_copy(ref, target, sems.at[n]))
        copies[-1].start()
        start += ref.shape[0]
    windows = h_ref.shape[0]
    wide = 16 * windows

    def centres(ref, shape):
        window = lax.broadcasted_iota(jnp.int32, shape, 1) // 16
        found = jnp.zeros(shape, jnp.int32)
        for w in range(windows):
            found = jnp.where(window == w, ref[w], found)
        return found

    block = 32
    below = lax.broadcasted_iota(jnp.int32, (block, wide), 0)
    freq_l = centres(l_ref, (block, wide)) + lax.rem(lax.broadcasted_iota(jnp.int32, (block, wide), 1), 16) - 8
    fine = turn(freq_l, below, depth)
    coarse = turn(freq_l, below * block, depth)
    shift_ref[0] = coarse[0]
    shift_ref[1] = coarse[1]
    for step in range(depth // block):
        now = times(fine, (shift_ref[0, step : step + 1], shift_ref[1, step : step + 1]))
        at = pl.ds(step * block, block)
        phase_ref[at, 0:wide] = now[0]
        phase_ref[at, wide : 2 * wide] = -now[1]
    table, left = split(phase_ref[0:depth])

    def dot(a, b):
        return jnp.dot(a, b, preferred_element_type=jnp.float32)

    for copy in copies:
        copy.wait()
    value, rest = split(grid_ref[...].reshape(rows_x * rows_y, depth))
    found = dot(value, table) + (dot(value, left) + dot(rest, table))
    along_z_ref[...] = found.reshape(rows_x, rows_y, 2 * wide)
    row16 = lax.broadcasted_iota(jnp.int32, (16, wide), 0)
    freq_k = centres(k_ref, (16, wide)) + row16 - 8
    now = turn(freq_k, place_ref[1] + 2 * total_y, total_y)
    step = turn(freq_k, 1, total_y)
    for y in range(rows_y):
        phase_ref[pl.ds(32 * y, 16), 0:wide] = now[0]
        phase_ref[pl.ds(32 * y + 16, 16), 0:wide] = now[1]
        now = times(now, step)
    group = 4
    for x in range(0, rows_x, group):
        real = [jnp.zeros((16, wide), jnp.float32)] * group
        imag = [jnp.zeros((16, wide), jnp.float32)] * group
        for y in range(rows_y):
            cos = phase_ref[pl.ds(32 * y, 16), 0:wide]
            sin = phase_ref[pl.ds(32 * y + 16, 16), 0:wide]
            for g in range(group):
                a = along_z_ref[x + g, y : y + 1, 0:wide]
                b = along_z_ref[x + g, y : y + 1, wide : 2 * wide]
                real[g] = real[g] + (a * cos + b * sin)
                imag[g] = imag[g] + (b * cos - a * sin)
        for g in range(group):
            half_ref[x + g, 0:16] = real[g]
            half_ref[x + g, 16:32] = imag[g]
    freq_h = centres(h_ref, (16, wide)) + row16 - 8
    now = turn(freq_h, place_ref[0] + 2 * total_x, total_x)
    step = turn(freq_h, 1, total_x)
    for x in range(rows_x):
        phase_ref[pl.ds(32 * x, 16), wide : 2 * wide] = now[0]
        phase_ref[pl.ds(32 * x + 16, 16), wide : 2 * wide] = now[1]
        now = times(now, step)
    for h in range(0, 16, group):
        real = [jnp.zeros((16, wide), jnp.float32)] * group
        imag = [jnp.zeros((16, wide), jnp.float32)] * group
        for x in range(rows_x):
            a = half_ref[x, 0:16]
            b = half_ref[x, 16:32]
            for g in range(group):
                cos = phase_ref[32 * x + h + g : 32 * x + h + g + 1, wide : 2 * wide]
                sin = phase_ref[32 * x + 16 + h + g : 32 * x + 17 + h + g, wide : 2 * wide]
                real[g] = real[g] + (a * cos + b * sin)
                imag[g] = imag[g] + (b * cos - a * sin)
        for g in range(group):
            wave_ref[pl.ds(32 * (h + g), 16)] = real[g]
            wave_ref[pl.ds(32 * (h + g) + 16, 16)] = imag[g]
    turned = jnp.transpose(wave_ref[...])
    pieces, _, lanes = out_ref.shape
    per_window = pieces // windows
    for piece in range(pieces):
        w, part = piece // per_window, piece % per_window
        out_ref[piece] = turned[16 * w : 16 * w + 16, part * lanes : (part + 1) * lanes]


def amplitude(grids, place, miller_h, miller_k, miller_l, total_x, total_y, pieces):
    _, rows_y, depth = grids[0].shape
    rows_x = sum(grid.shape[0] for grid in grids)
    windows = miller_h.shape[0]
    wide = 16 * windows
    vmem = pl.BlockSpec(memory_space=pltpu.VMEM)
    far = pl.BlockSpec(memory_space=pl.ANY)
    smem = pl.BlockSpec(memory_space=pltpu.SMEM)
    return pl.pallas_call(
        functools.partial(amplitude_body, total_x=total_x, total_y=total_y),
        in_specs=[smem, smem, smem, smem, far, far, far],
        out_specs=vmem,
        out_shape=jax.ShapeDtypeStruct((pieces, 16, 32 * wide // pieces), jnp.float32),
        scratch_shapes=[
            pltpu.VMEM((max(depth, 32 * rows_y, 32 * rows_x), 2 * wide), jnp.float32),
            pltpu.VMEM((2, 32, wide), jnp.float32),
            pltpu.VMEM((rows_x, rows_y, 2 * wide), jnp.float32),
            pltpu.VMEM((rows_x, 32, wide), jnp.float32),
            pltpu.VMEM((512, wide), jnp.float32),
            pltpu.VMEM((rows_x, rows_y, depth), jnp.float32),
            pltpu.SemaphoreType.DMA((3,)),
        ],
        compiler_params=pltpu.CompilerParams(vmem_limit_bytes=62 << 20),
        cost_estimate=pl.CostEstimate(flops=5_000_000_000, bytes_accessed=8_000_000, transcendentals=100_000),
    )(place, miller_h, miller_k, miller_l, *grids)


def exchange(head, tail, axis):
    count = lax.axis_size(axis)
    before = lax.ppermute(tail, axis, [(i, (i + 1) % count) for i in range(count)])
    after = lax.ppermute(head, axis, [((i + 1) % count, i) for i in range(count)])
    return before, after


def added(inner, before, after, dim):
    length = inner.shape[dim]
    widths = [(0, 0)] * inner.ndim
    widths[dim] = (0, length - 4)
    leading = jnp.pad(before, widths)
    widths[dim] = (length - 4, 0)
    return inner + leading + jnp.pad(after, widths)


def shards(atom_cell, atom_frac, atom_weight, block_count, miller_h, miller_k, miller_l):
    blocks_x, blocks_y, blocks_z, _ = atom_weight.shape
    count_x, count_y = lax.axis_size("gx"), lax.axis_size("gy")
    width_x, width_y, depth = 8 * blocks_x, 8 * blocks_y, 8 * blocks_z
    total_x, total_y = width_x * count_x, width_y * count_y
    place = jnp.stack([lax.axis_index("gx") * width_x - 4, lax.axis_index("gy") * width_y - 4])
    grids = deposit(atom_cell, atom_frac, atom_weight, block_count)
    head, mid, tail = grids
    before, after = exchange(head, tail, "gx")
    pieces = count_x * count_y
    waves = amplitude(
        grids, place.astype(jnp.int32), miller_h, miller_k, miller_l, total_x, total_y, pieces
    )
    before, after, _ = lax.optimization_barrier((before, after, waves))
    received = lax.all_to_all(waves, ("gx", "gy"), 0, 0, tiled=False)
    rows = miller_h.shape[0] * 16 // pieces
    summed = jnp.sum(received, axis=0).reshape(16, rows, 2, 16)
    power = jnp.sum(summed * summed, axis=2) / float(total_x * total_y * depth)
    intensity = jnp.transpose(power, (1, 2, 0)).reshape(rows, 256)
    wide = added(mid, before, after, 0)
    before, after = exchange(wide[:, :4], wide[:, width_y + 4 :], "gy")
    density = added(wide[:, 4 : width_y + 4], before, after, 1)
    return (density, intensity)


def solution(mesh):
    in_specs = (
        P(None, "gx", "gy", None, None),
        P(None, "gx", "gy", None, None),
        P("gx", "gy", None, None),
        P("gx", "gy", None),
        P(),
        P(),
        P(),
    )
    out_specs = (P("gx", "gy", None), P(("gx", "gy"), None))
    return jax.shard_map(shards, mesh=mesh, in_specs=in_specs, out_specs=out_specs, check_vma=False)
```

```python
import functools
import math

import jax
import jax.numpy as jnp
from jax import lax
from jax.experimental import pallas as pl
from jax.experimental.pallas import tpu as pltpu
from jax.sharding import PartitionSpec as P

KERNEL_SIGMA = 0.9
NORMAL = 1.0 / (KERNEL_SIGMA * math.sqrt(2.0 * math.pi))
SCALE = math.sqrt(0.5 / math.log(2.0)) / KERNEL_SIGMA
LOG_NORMAL = math.log2(NORMAL)
FAR = -1.0e4
LANES_BY_LANES = (((1,), (1,)), ((), ()))
UNROLL = 32
FINE = 32


def turn(freqs, place, extent):
    product = freqs * place
    if extent & (extent - 1) == 0:
        product = product & (extent - 1)
    else:
        product = lax.rem(lax.rem(product, extent) + extent, extent)
    if extent & (extent - 1) or extent < 8:
        angle = product.astype(jnp.float32) * (2.0 * math.pi / extent)
        return jnp.cos(angle), jnp.sin(angle)
    quarters = (product + extent // 8) >> ((extent // 4).bit_length() - 1)
    angle = (product - quarters * (extent // 4)).astype(jnp.float32) * (2.0 * math.pi / extent)
    square = angle * angle
    cos = jnp.full_like(angle, -1.0 / math.factorial(10))
    for n in (8, 6, 4, 2, 0):
        cos = cos * square + (-1.0) ** (n // 2) / math.factorial(n)
    sin = jnp.full_like(angle, 1.0 / math.factorial(9))
    for n in (7, 5, 3, 1):
        sin = sin * square + (-1.0) ** (n // 2) / math.factorial(n)
    sin = sin * angle
    odd = (quarters & 1) == 1
    cos, sin = jnp.where(odd, sin, cos), jnp.where(odd, cos, sin)
    cos = jnp.where(((quarters + 1) & 2) == 2, -cos, cos)
    return cos, jnp.where((quarters & 2) == 2, -sin, sin)


def times(one, other):
    return (
        one[0] * other[0] - one[1] * other[1],
        one[0] * other[1] + one[1] * other[0],
    )


def split(value):
    head = value.astype(jnp.bfloat16)
    return head, (value - head.astype(jnp.float32)).astype(jnp.bfloat16)


def phase_tables(place, millers, extents, shift_ref, table_ref, phase_y_ref, phase_x_ref):
    h_ref, k_ref, l_ref = millers
    total_x, total_y, depth = extents
    windows = h_ref.shape[0]
    wide = 16 * windows

    def centres(ref, rows):
        window = lax.broadcasted_iota(jnp.int32, (rows, wide), 1) // 16
        found = jnp.zeros((rows, wide), jnp.int32)
        for w in range(windows):
            found = jnp.where(window == w, ref[w], found)
        return found - 8

    lane = lax.broadcasted_iota(jnp.int32, (FINE, wide), 1) % 16
    below = lax.broadcasted_iota(jnp.int32, (FINE, wide), 0)
    freq_l = centres(l_ref, FINE) + lane
    fine = turn(freq_l, below, depth)
    coarse = turn(freq_l, below * FINE, depth)
    shift_ref[0] = coarse[0]
    shift_ref[1] = coarse[1]
    for step in range(depth // FINE):
        now = times(fine, (shift_ref[0, step : step + 1], shift_ref[1, step : step + 1]))
        at = pl.ds(step * FINE, FINE)
        for side, value in ((0, now[0]), (1, -now[1])):
            head, rest = split(value)
            table_ref[0, at, side * wide : (side + 1) * wide] = head
            table_ref[1, at, side * wide : (side + 1) * wide] = rest
    row = lax.broadcasted_iota(jnp.int32, (16, wide), 0)
    for ref, out_ref, start, total in (
        (k_ref, phase_y_ref, place[1], total_y),
        (h_ref, phase_x_ref, place[0], total_x),
    ):
        freqs = centres(ref, 16) + row
        now = turn(freqs, start + 2 * total, total)
        step = turn(freqs, 1, total)
        for n in range(out_ref.shape[0]):
            out_ref[n, 0:16] = now[0]
            out_ref[n, 16:32] = now[1]
            now = times(now, step)


def transforms(grid_ref, table_ref, phase_y_ref, phase_x_ref, along_z_ref, half_ref, wave_ref, out_ref, late):
    rows_x, rows_y, depth = grid_ref.shape
    wide = wave_ref.shape[1]

    def dot(a, b):
        return jnp.dot(a, b, preferred_element_type=jnp.float32)

    value, rest = split(grid_ref[...].reshape(rows_x * rows_y, depth))
    found = dot(value, table_ref[0]) + (dot(value, table_ref[1]) + dot(rest, table_ref[0]))
    along_z_ref[...] = found.reshape(rows_x, rows_y, 2 * wide)
    for copy in late:
        copy.wait()
    group = 5 if rows_x % 5 == 0 else 1
    for x in range(0, rows_x, group):
        real = [jnp.zeros((16, wide), jnp.float32)] * group
        imag = [jnp.zeros((16, wide), jnp.float32)] * group
        for y in range(1, rows_y):
            cos = phase_y_ref[y, 0:16]
            sin = phase_y_ref[y, 16:32]
            for g in range(group):
                a = along_z_ref[x + g, y : y + 1, 0:wide]
                b = along_z_ref[x + g, y : y + 1, wide : 2 * wide]
                real[g] = real[g] + (a * cos + b * sin)
                imag[g] = imag[g] + (b * cos - a * sin)
        for g in range(group):
            half_ref[x + g, 0:16] = real[g]
            half_ref[x + g, 16:32] = imag[g]
    group = 4
    for h in range(0, 16, group):
        real = [jnp.zeros((16, wide), jnp.float32)] * group
        imag = [jnp.zeros((16, wide), jnp.float32)] * group
        for x in range(rows_x):
            a = half_ref[x, 0:16]
            b = half_ref[x, 16:32]
            for g in range(group):
                cos = phase_x_ref[x, h + g : h + g + 1]
                sin = phase_x_ref[x, 16 + h + g : 17 + h + g]
                real[g] = real[g] + (a * cos + b * sin)
                imag[g] = imag[g] + (b * cos - a * sin)
        for g in range(group):
            wave_ref[pl.ds(32 * (h + g), 16)] = real[g]
            wave_ref[pl.ds(32 * (h + g) + 16, 16)] = imag[g]
    turned = jnp.transpose(wave_ref[...])
    pieces, _, lanes = out_ref.shape
    per_window = pieces // (wide // 16)
    for piece in range(pieces):
        w, part = piece // per_window, piece % per_window
        out_ref[piece] = turned[16 * w : 16 * w + 16, part * lanes : (part + 1) * lanes]


def deposit_column(column, fetches, next_fetches, cell_ref, frac_ref, weight_ref, count_ref, rows_ref, edge_ref, line_ref):
    cap, blocks_z = weight_ref.shape
    depth = 8 * blocks_z
    half = blocks_z // 2
    two = 2 * cap

    def paired(value):
        value = jnp.transpose(value)
        return jnp.concatenate([value[:half], value[half:]], axis=1).reshape(half // UNROLL, UNROLL, two)

    line_ref[...] = jnp.zeros_like(line_ref)
    for d in range(3):
        fetches[2 * d].wait()
        fetches[2 * d + 1].wait()
        cell = cell_ref[d].astype(jnp.float32)
        place = cell + frac_ref[d]
        if d == 0:
            upper = jnp.where(cell > 3.5, 1.0, 0.0)
            rows_ref[0] = paired((place - 3.5) * SCALE)
            rows_ref[1] = paired(upper)
            rows_ref[2] = paired(cell - 4.0 * upper)
        else:
            rows_ref[2 * d + 1] = paired(place * SCALE)
            rows_ref[2 * d + 2] = paired(cell)
    fetches[6].wait()
    slots = lax.broadcasted_iota(jnp.int32, (cap, blocks_z), 0)
    rows_ref[7] = paired(jnp.where(slots < count_ref[0, pl.ds(column, 1), :], weight_ref[...], 0.0))
    next_fetches()
    row = lax.broadcasted_iota(jnp.int32, (8, 128), 0)
    row8 = row.astype(jnp.float32)
    low = (row8 - 4.0) * SCALE
    high = (row8 + 4.0) * SCALE
    row4 = (row % 4).astype(jnp.float32)
    second = row >= 4
    nodes = (4.0 * row4 - 6.0) * SCALE
    first = jnp.where(second, 1.0, 0.0)
    on_lower = jnp.where((row4 >= first) & (row4 <= first + 1.0), 0.0, FAR)
    on_upper = jnp.where((row4 >= first + 1.0) & (row4 <= first + 2.0), 0.0, FAR)
    slopes = (row4 - 1.5) * (2.0 * SCALE)
    sign = jnp.where(second, -1.0, 1.0)
    bound = jnp.where(second, 0.5 - row4, row4)
    part = cap % 128
    lanes = lax.broadcasted_iota(jnp.int32, (16, 128), 1)
    none = jnp.zeros((16, 128), jnp.bfloat16)

    def group(g, carry):
        for u in range(UNROLL):
            lefts = [[], []]
            rights = [[], []]
            for t in range(two // 128):

                def line(k):
                    return rows_ref[k, g, u : u + 1, 128 * t : 128 * t + 128]

                def taps(d):
                    inside = row8 > line(2 * d + 2)
                    away = jnp.where(inside, low, high) - line(2 * d + 1)
                    return inside, jnp.exp2(LOG_NORMAL - away * away)

                def halves(inside, value):
                    return jnp.concatenate([jnp.where(inside, value, 0.0), jnp.where(inside, 0.0, value)], axis=0)

                here = (u % 2) * (two // 128) + t
                place = line(0)
                away = place - nodes
                edge_ref[here, 0:8] = jnp.exp2(jnp.where(line(1) > 0.5, on_upper, on_lower) - away * away)
                edge_ref[here, 8:16] = jnp.exp2(jnp.where(bound > sign * line(2), slopes * place, FAR))
                inside, value = taps(1)
                taps_y = halves(inside, value)
                inside, value = taps(2)
                scaled = halves(inside, value * line(7))

                def rows(values, start, dead):
                    sides = []
                    for s in range(2):
                        sides.append(
                            jnp.concatenate(
                                [
                                    none
                                    if (s, n) in dead
                                    else (
                                        values * edge_ref[here, start + 4 * s + n : start + 4 * s + n + 1, :]
                                    ).astype(jnp.bfloat16)
                                    for n in range(4)
                                ],
                                axis=0,
                            )
                        )
                    return jnp.concatenate(sides, axis=1)

                right = rows(taps_y, 8, [(0, 0)])
                if part and t == cap // 128:
                    owned = [(0, jnp.where(lanes < part, scaled, 0.0)), (1, jnp.where(lanes < part, 0.0, scaled))]
                else:
                    owned = [(int(128 * t >= cap), scaled)]
                for side, values in owned:
                    lefts[side].append(rows(values, 0, [(0, 3), (1, 0)]))
                    rights[side].append(right)
            base = pl.multiple_of(8 * (g * UNROLL + u), 8)
            for s in range(2):
                found = lax.dot_general(
                    jnp.concatenate(lefts[s], axis=1),
                    jnp.concatenate(rights[s], axis=1),
                    LANES_BY_LANES,
                    preferred_element_type=jnp.float32,
                )
                for n in range(4):
                    line_ref[n, pl.ds(base + 8 * half * s, 16), :] += found[16 * n : 16 * n + 16]
        return carry

    lax.fori_loop(0, half // UNROLL, group, 0)


def add_column(column, line_ref, grid_ref, finished):
    depth = grid_ref.shape[2]
    for n in range(4):
        line_ref[n, 4:8, :] += line_ref[n, depth + 4 : depth + 8, :]
        line_ref[n, depth : depth + 4, :] += line_ref[n, 0:4, :]
    at = pl.ds(pl.multiple_of(8 * column, 8), 16)
    for n in range(4):
        for c in range(depth // 128):
            turned = jnp.transpose(line_ref[n, 128 * c + 4 : 128 * c + 132, :])
            for k in range(4):
                near = k - 1.5
                factor = NORMAL * math.exp((-near * (4 * n - 6) - 0.5 * near * near) / KERNEL_SIGMA**2)
                grid_ref[4 * n + k, at, 128 * c : 128 * c + 128] += turned[16 * k : 16 * k + 16] * factor
        finished(n)


def deposit_body(
    h_ref, k_ref, l_ref, count_ref, cell_ref, frac_ref, weight_ref,
    head_ref, mid_ref, tail_ref, table_out_ref, phase_y_out_ref, phase_x_out_ref,
    cells_ref, fracs_ref, weights_ref, rows_ref, edge_ref, line_ref, grid_ref, shift_ref,
    table_ref, phase_y_ref, phase_x_ref, in_sems, out_sems, *, totals,
):
    columns = weights_ref.shape[0]
    rows_x, rows_y, depth = grid_ref.shape

    def fetches(j):
        found = []
        for d in range(3):
            found.append(pltpu.make_async_copy(cell_ref.at[d, 0, j], cells_ref.at[j, d], in_sems.at[j, 2 * d]))
            found.append(pltpu.make_async_copy(frac_ref.at[d, 0, j], fracs_ref.at[j, d], in_sems.at[j, 2 * d + 1]))
        found.append(pltpu.make_async_copy(weight_ref.at[0, j], weights_ref.at[j], in_sems.at[j, 6]))
        return found

    for copy in fetches(0):
        copy.start()
    place = (lax.axis_index("gx") * (rows_x - 8) - 3, lax.axis_index("gy") * (rows_y - 8) - 4)
    phase_tables(
        place, (h_ref, k_ref, l_ref), (*totals, depth), shift_ref, table_ref, phase_y_ref, phase_x_ref
    )
    leaving = [
        pltpu.make_async_copy(table_ref, table_out_ref, out_sems.at[0]),
        pltpu.make_async_copy(phase_y_ref, phase_y_out_ref, out_sems.at[1]),
        pltpu.make_async_copy(phase_x_ref, phase_x_out_ref, out_sems.at[2]),
    ]
    for copy in leaving:
        copy.start()
    grid_ref[...] = jnp.zeros_like(grid_ref)

    def column(j, carry):
        def next_fetches():
            @pl.when(j < columns - 1)
            def _():
                for copy in fetches(j + 1):
                    copy.start()

        deposit_column(
            j, fetches(j), next_fetches, cells_ref.at[j], fracs_ref.at[j], weights_ref.at[j], count_ref, rows_ref, edge_ref, line_ref
        )

        @pl.when(j < columns - 1)
        def _():
            add_column(j, line_ref, grid_ref, lambda n: None)

        return carry

    lax.fori_loop(0, columns, column, 0)

    def finished(n):
        if n != 1:
            face, start = {0: (head_ref, 1), 2: (mid_ref, 4), 3: (tail_ref, 12)}[n]
            copy = pltpu.make_async_copy(
                grid_ref.at[pl.ds(start, face.shape[0])], face, out_sems.at[len(leaving)]
            )
            copy.start()
            leaving.append(copy)

    add_column(columns - 1, line_ref, grid_ref, finished)
    for copy in leaving:
        copy.wait()


def transform_body(
    head_ref, mid_ref, tail_ref, table_in_ref, phase_y_in_ref, phase_x_in_ref, out_ref,
    grid_ref, table_ref, phase_y_ref, phase_x_ref, along_z_ref, half_ref, wave_ref, sems,
):
    faces = []
    start = 0
    for n, ref in enumerate((head_ref, mid_ref, tail_ref)):
        faces.append(pltpu.make_async_copy(ref, grid_ref.at[pl.ds(start, ref.shape[0])], sems.at[n]))
        start += ref.shape[0]
    tables = [
        pltpu.make_async_copy(table_in_ref, table_ref, sems.at[3]),
        pltpu.make_async_copy(phase_y_in_ref, phase_y_ref, sems.at[4]),
        pltpu.make_async_copy(phase_x_in_ref, phase_x_ref, sems.at[5]),
    ]
    tables[0].start()
    for copy in faces:
        copy.start()
    for copy in tables[1:]:
        copy.start()
    tables[0].wait()
    for copy in faces:
        copy.wait()
    transforms(grid_ref, table_ref, phase_y_ref, phase_x_ref, along_z_ref, half_ref, wave_ref, out_ref, tables[1:])


FAR_AWAY = pl.BlockSpec(memory_space=pl.ANY)
NEARBY = pl.BlockSpec(memory_space=pltpu.VMEM)


def deposit(cell, frac, weight, count, miller_h, miller_k, miller_l, totals):
    _, columns, blocks_z, cap = weight.shape
    depth = 8 * blocks_z
    rows_x, rows_y = 16, 8 * columns + 8
    wide = 16 * miller_h.shape[0]

    def turned(value):
        return jnp.swapaxes(value, -1, -2)

    smem = pl.BlockSpec(memory_space=pltpu.SMEM)
    f32 = jnp.float32
    tables = [((2, depth, 2 * wide), jnp.bfloat16), ((rows_y, 32, wide), f32), ((rows_x - 1, 32, wide), f32)]
    return pl.pallas_call(
        functools.partial(deposit_body, totals=totals),
        in_specs=[smem, smem, smem, NEARBY, FAR_AWAY, FAR_AWAY, FAR_AWAY],
        out_specs=[FAR_AWAY] * 6,
        out_shape=[jax.ShapeDtypeStruct((n, rows_y, depth), f32) for n in (3, 8, 4)]
        + [jax.ShapeDtypeStruct(*table) for table in tables],
        scratch_shapes=[
            pltpu.VMEM((columns, 3, cap, blocks_z), jnp.int32),
            pltpu.VMEM((columns, 3, cap, blocks_z), f32),
            pltpu.VMEM((columns, cap, blocks_z), f32),
            pltpu.VMEM((8, blocks_z // 2 // UNROLL, UNROLL, 2 * cap), f32),
            pltpu.VMEM((2 * (2 * cap // 128), 16, 128), f32),
            pltpu.VMEM((4, depth + 8, 64), f32),
            pltpu.VMEM((rows_x, rows_y, depth), f32),
            pltpu.VMEM((2, depth // FINE, wide), f32),
            *[pltpu.VMEM(*table) for table in tables],
            pltpu.SemaphoreType.DMA((columns, 7)),
            pltpu.SemaphoreType.DMA((6,)),
        ],
        compiler_params=pltpu.CompilerParams(vmem_limit_bytes=60 << 20),
    )(miller_h, miller_k, miller_l, count, turned(cell), turned(frac), turned(weight))


def transform(faces, tables, pieces):
    _, rows_y, depth = faces[0].shape
    rows_x = sum(face.shape[0] for face in faces)
    wide = tables[1].shape[2]
    f32 = jnp.float32
    return pl.pallas_call(
        transform_body,
        in_specs=[FAR_AWAY] * 6,
        out_specs=NEARBY,
        out_shape=jax.ShapeDtypeStruct((pieces, 16, 32 * wide // pieces), f32),
        scratch_shapes=[
            pltpu.VMEM((rows_x, rows_y, depth), f32),
            *[pltpu.VMEM(table.shape, table.dtype) for table in tables],
            pltpu.VMEM((rows_x, rows_y, 2 * wide), f32),
            pltpu.VMEM((rows_x, 32, wide), f32),
            pltpu.VMEM((512, wide), f32),
            pltpu.SemaphoreType.DMA((6,)),
        ],
        compiler_params=pltpu.CompilerParams(vmem_limit_bytes=60 << 20),
        cost_estimate=pl.CostEstimate(flops=5_000_000_000, bytes_accessed=8_000_000, transcendentals=0),
    )(*faces, *tables)


def exchange(head, tail, axis):
    count = lax.axis_size(axis)
    before = lax.ppermute(tail, axis, [(i, (i + 1) % count) for i in range(count)])
    after = lax.ppermute(head, axis, [((i + 1) % count, i) for i in range(count)])
    return before, after


def added(inner, before, after, dim):
    length = inner.shape[dim]
    widths = [(0, 0)] * inner.ndim
    widths[dim] = (0, length - before.shape[dim])
    leading = jnp.pad(before, widths)
    widths[dim] = (length - after.shape[dim], 0)
    return inner + leading + jnp.pad(after, widths)


def shards(atom_cell, atom_frac, atom_weight, block_count, miller_h, miller_k, miller_l):
    blocks_x, blocks_y, blocks_z, _ = atom_weight.shape
    count_x, count_y = lax.axis_size("gx"), lax.axis_size("gy")
    width_x, width_y, depth = 8 * blocks_x, 8 * blocks_y, 8 * blocks_z
    total_x, total_y = width_x * count_x, width_y * count_y
    pieces = count_x * count_y
    head, mid, tail, *tables = deposit(
        atom_cell, atom_frac, atom_weight, block_count, miller_h, miller_k, miller_l, (total_x, total_y)
    )
    before, after = exchange(head, tail, "gx")
    waves = transform((head, mid, tail), tables, pieces)
    before, after, _ = lax.optimization_barrier((before, after, waves))
    received = lax.all_to_all(waves, ("gx", "gy"), 0, 0, tiled=False)
    rows = miller_h.shape[0] * 16 // pieces
    summed = jnp.sum(received, axis=0).reshape(16, rows, 2, 16)
    power = jnp.sum(summed * summed, axis=2) / float(total_x * total_y * depth)
    intensity = jnp.transpose(power, (1, 2, 0)).reshape(rows, 256)
    wide = added(mid, before, after, 0)
    before, after = exchange(wide[:, :4], wide[:, width_y + 4 :], "gy")
    density = added(wide[:, 4 : width_y + 4], before, after, 1)
    return (density, intensity)


def solution(mesh):
    in_specs = (
        P(None, "gx", "gy", None, None),
        P(None, "gx", "gy", None, None),
        P("gx", "gy", None, None),
        P("gx", "gy", None),
        P(),
        P(),
        P(),
    )
    out_specs = (P("gx", "gy", None), P(("gx", "gy"), None))
    return jax.shard_map(shards, mesh=mesh, in_specs=in_specs, out_specs=out_specs, check_vma=False)
```

```python
import functools
import math

import jax
import jax.numpy as jnp
from jax import lax
from jax.experimental import pallas as pl
from jax.experimental.pallas import tpu as pltpu
from jax.sharding import PartitionSpec as P

KERNEL_SIGMA = 0.9
NORMAL = 1.0 / (KERNEL_SIGMA * math.sqrt(2.0 * math.pi))
SCALE = math.sqrt(0.5 / math.log(2.0)) / KERNEL_SIGMA
LOG_NORMAL = math.log2(NORMAL)
FAR = -1.0e4
LANES_BY_LANES = (((1,), (1,)), ((), ()))
UNROLL = 32
FINE = 32


def turn(freqs, place, extent):
    product = freqs * place
    if extent & (extent - 1) == 0:
        product = product & (extent - 1)
    else:
        product = lax.rem(lax.rem(product, extent) + extent, extent)
    if extent & (extent - 1) or extent < 8:
        angle = product.astype(jnp.float32) * (2.0 * math.pi / extent)
        return jnp.cos(angle), jnp.sin(angle)
    quarters = (product + extent // 8) >> ((extent // 4).bit_length() - 1)
    angle = (product - quarters * (extent // 4)).astype(jnp.float32) * (2.0 * math.pi / extent)
    square = angle * angle
    cos = jnp.full_like(angle, -1.0 / math.factorial(10))
    for n in (8, 6, 4, 2, 0):
        cos = cos * square + (-1.0) ** (n // 2) / math.factorial(n)
    sin = jnp.full_like(angle, 1.0 / math.factorial(9))
    for n in (7, 5, 3, 1):
        sin = sin * square + (-1.0) ** (n // 2) / math.factorial(n)
    sin = sin * angle
    odd = (quarters & 1) == 1
    cos, sin = jnp.where(odd, sin, cos), jnp.where(odd, cos, sin)
    cos = jnp.where(((quarters + 1) & 2) == 2, -cos, cos)
    return cos, jnp.where((quarters & 2) == 2, -sin, sin)


def times(one, other):
    return (
        one[0] * other[0] - one[1] * other[1],
        one[0] * other[1] + one[1] * other[0],
    )


def split(value):
    head = value.astype(jnp.bfloat16)
    return head, (value - head.astype(jnp.float32)).astype(jnp.bfloat16)


def phase_tables(place, millers, extents, shift_ref, table_ref, phase_y_ref, phase_x_ref):
    h_ref, k_ref, l_ref = millers
    total_x, total_y, depth = extents
    windows = h_ref.shape[0]
    wide = 16 * windows

    def centres(ref, rows):
        window = lax.broadcasted_iota(jnp.int32, (rows, wide), 1) // 16
        found = jnp.zeros((rows, wide), jnp.int32)
        for w in range(windows):
            found = jnp.where(window == w, ref[w], found)
        return found - 8

    lane = lax.broadcasted_iota(jnp.int32, (FINE, wide), 1) % 16
    below = lax.broadcasted_iota(jnp.int32, (FINE, wide), 0)
    freq_l = centres(l_ref, FINE) + lane
    fine = turn(freq_l, below, depth)
    coarse = turn(freq_l, below * FINE, depth)
    shift_ref[0] = coarse[0]
    shift_ref[1] = coarse[1]
    for step in range(depth // FINE):
        now = times(fine, (shift_ref[0, step : step + 1], shift_ref[1, step : step + 1]))
        at = pl.ds(step * FINE, FINE)
        for side, value in ((0, now[0]), (1, -now[1])):
            head, rest = split(value)
            table_ref[0, at, side * wide : (side + 1) * wide] = head
            table_ref[1, at, side * wide : (side + 1) * wide] = rest
    row = lax.broadcasted_iota(jnp.int32, (16, wide), 0)
    for ref, out_ref, start, total in (
        (k_ref, phase_y_ref, place[1], total_y),
        (h_ref, phase_x_ref, place[0], total_x),
    ):
        freqs = centres(ref, 16) + row
        now = turn(freqs, start + 2 * total, total)
        step = turn(freqs, 1, total)
        for n in range(out_ref.shape[0]):
            out_ref[n, 0:16] = now[0]
            out_ref[n, 16:32] = now[1]
            now = times(now, step)


def transforms(grid_ref, table_ref, phase_y_ref, phase_x_ref, along_z_ref, half_ref, wave_ref, out_ref):
    rows_x, rows_y, depth = grid_ref.shape
    wide = wave_ref.shape[1]

    def dot(a, b):
        return jnp.dot(a, b, preferred_element_type=jnp.float32)

    value, rest = split(grid_ref[...].reshape(rows_x * rows_y, depth))
    found = dot(value, table_ref[0]) + (dot(value, table_ref[1]) + dot(rest, table_ref[0]))
    along_z_ref[...] = found.reshape(rows_x, rows_y, 2 * wide)
    group = 5 if rows_x % 5 == 0 else 1
    for x in range(0, rows_x, group):
        real = [jnp.zeros((16, wide), jnp.float32)] * group
        imag = [jnp.zeros((16, wide), jnp.float32)] * group
        for y in range(1, rows_y):
            cos = phase_y_ref[y, 0:16]
            sin = phase_y_ref[y, 16:32]
            for g in range(group):
                a = along_z_ref[x + g, y : y + 1, 0:wide]
                b = along_z_ref[x + g, y : y + 1, wide : 2 * wide]
                real[g] = real[g] + (a * cos + b * sin)
                imag[g] = imag[g] + (b * cos - a * sin)
        for g in range(group):
            half_ref[x + g, 0:16] = real[g]
            half_ref[x + g, 16:32] = imag[g]
    group = 4
    for h in range(0, 16, group):
        real = [jnp.zeros((16, wide), jnp.float32)] * group
        imag = [jnp.zeros((16, wide), jnp.float32)] * group
        for x in range(rows_x):
            a = half_ref[x, 0:16]
            b = half_ref[x, 16:32]
            for g in range(group):
                cos = phase_x_ref[x, h + g : h + g + 1]
                sin = phase_x_ref[x, 16 + h + g : 17 + h + g]
                real[g] = real[g] + (a * cos + b * sin)
                imag[g] = imag[g] + (b * cos - a * sin)
        for g in range(group):
            wave_ref[pl.ds(32 * (h + g), 16)] = real[g]
            wave_ref[pl.ds(32 * (h + g) + 16, 16)] = imag[g]
    turned = jnp.transpose(wave_ref[...])
    pieces, _, lanes = out_ref.shape
    per_window = pieces // (wide // 16)
    for piece in range(pieces):
        w, part = piece // per_window, piece % per_window
        out_ref[piece] = turned[16 * w : 16 * w + 16, part * lanes : (part + 1) * lanes]


def deposit_column(column, cell_ref, frac_ref, weight_ref, count_ref, rows_ref, edge_ref, line_ref):
    cap, blocks_z = weight_ref.shape
    depth = 8 * blocks_z
    half = blocks_z // 2
    two = 2 * cap

    def paired(value):
        value = jnp.transpose(value)
        return jnp.concatenate([value[:half], value[half:]], axis=1).reshape(half // UNROLL, UNROLL, two)

    line_ref[...] = jnp.zeros_like(line_ref)
    for d in range(3):
        cell = cell_ref[d].astype(jnp.float32)
        place = cell + frac_ref[d]
        if d == 0:
            upper = jnp.where(cell > 3.5, 1.0, 0.0)
            rows_ref[0] = paired((place - 3.5) * SCALE)
            rows_ref[1] = paired(upper)
            rows_ref[2] = paired(cell - 4.0 * upper)
        else:
            rows_ref[2 * d + 1] = paired(place * SCALE)
            rows_ref[2 * d + 2] = paired(cell)
    slots = lax.broadcasted_iota(jnp.int32, (cap, blocks_z), 0)
    rows_ref[7] = paired(jnp.where(slots < count_ref[0, pl.ds(column, 1), :], weight_ref[...], 0.0))
    row = lax.broadcasted_iota(jnp.int32, (8, 128), 0)
    row8 = row.astype(jnp.float32)
    low = (row8 - 4.0) * SCALE
    high = (row8 + 4.0) * SCALE
    row4 = (row % 4).astype(jnp.float32)
    second = row >= 4
    nodes = (4.0 * row4 - 6.0) * SCALE
    first = jnp.where(second, 1.0, 0.0)
    on_lower = jnp.where((row4 >= first) & (row4 <= first + 1.0), 0.0, FAR)
    on_upper = jnp.where((row4 >= first + 1.0) & (row4 <= first + 2.0), 0.0, FAR)
    slopes = (row4 - 1.5) * (2.0 * SCALE)
    sign = jnp.where(second, -1.0, 1.0)
    bound = jnp.where(second, 0.5 - row4, row4)
    part = cap % 128
    lanes = lax.broadcasted_iota(jnp.int32, (16, 128), 1)
    none = jnp.zeros((16, 128), jnp.bfloat16)

    def group(g, carry):
        for u in range(UNROLL):
            lefts = [[], []]
            rights = [[], []]
            for t in range(two // 128):

                def line(k):
                    return rows_ref[k, g, u : u + 1, 128 * t : 128 * t + 128]

                def taps(d):
                    inside = row8 > line(2 * d + 2)
                    away = jnp.where(inside, low, high) - line(2 * d + 1)
                    return inside, jnp.exp2(LOG_NORMAL - away * away)

                def halves(inside, value):
                    return jnp.concatenate([jnp.where(inside, value, 0.0), jnp.where(inside, 0.0, value)], axis=0)

                here = (u % 2) * (two // 128) + t
                place = line(0)
                away = place - nodes
                edge_ref[here, 0:8] = jnp.exp2(jnp.where(line(1) > 0.5, on_upper, on_lower) - away * away)
                edge_ref[here, 8:16] = jnp.exp2(jnp.where(bound > sign * line(2), slopes * place, FAR))
                inside, value = taps(1)
                taps_y = halves(inside, value)
                inside, value = taps(2)
                scaled = halves(inside, value * line(7))

                def rows(values, start, dead):
                    sides = []
                    for s in range(2):
                        sides.append(
                            jnp.concatenate(
                                [
                                    none
                                    if (s, n) in dead
                                    else (
                                        values * edge_ref[here, start + 4 * s + n : start + 4 * s + n + 1, :]
                                    ).astype(jnp.bfloat16)
                                    for n in range(4)
                                ],
                                axis=0,
                            )
                        )
                    return jnp.concatenate(sides, axis=1)

                right = rows(taps_y, 8, [(0, 0)])
                if part and t == cap // 128:
                    owned = [(0, jnp.where(lanes < part, scaled, 0.0)), (1, jnp.where(lanes < part, 0.0, scaled))]
                else:
                    owned = [(int(128 * t >= cap), scaled)]
                for side, values in owned:
                    lefts[side].append(rows(values, 0, [(0, 3), (1, 0)]))
                    rights[side].append(right)
            base = pl.multiple_of(8 * (g * UNROLL + u), 8)
            for s in range(2):
                found = lax.dot_general(
                    jnp.concatenate(lefts[s], axis=1),
                    jnp.concatenate(rights[s], axis=1),
                    LANES_BY_LANES,
                    preferred_element_type=jnp.float32,
                )
                for n in range(4):
                    line_ref[n, pl.ds(base + 8 * half * s, 16), :] += found[16 * n : 16 * n + 16]
        return carry

    lax.fori_loop(0, half // UNROLL, group, 0)


def add_column(column, line_ref, faces):
    depth = faces[0].shape[2]
    for n in range(4):
        line_ref[n, 4:8, :] += line_ref[n, depth + 4 : depth + 8, :]
        line_ref[n, depth : depth + 4, :] += line_ref[n, 0:4, :]
    at = pl.ds(pl.multiple_of(8 * column, 8), 16)
    for n in range(4):
        for c in range(depth // 128):
            turned = jnp.transpose(line_ref[n, 128 * c + 4 : 128 * c + 132, :])
            for k in range(4):
                near = k - 1.5
                factor = NORMAL * math.exp((-near * (4 * n - 6) - 0.5 * near * near) / KERNEL_SIGMA**2)
                face = faces[(n + 1) // 2]
                row = 4 * n + k - (1, 4, 12)[(n + 1) // 2]
                if row >= 0:
                    face[row, at, 128 * c : 128 * c + 128] += turned[16 * k : 16 * k + 16] * factor


def deposit_body(count_ref, cell_ref, frac_ref, weight_ref, head_ref, mid_ref, tail_ref, rows_ref, edge_ref, line_ref):
    column = pl.program_id(0)
    faces = (head_ref, mid_ref, tail_ref)

    @pl.when(column == 0)
    def _():
        for face in faces:
            face[...] = jnp.zeros_like(face)

    deposit_column(
        column, cell_ref.at[:, 0, 0], frac_ref.at[:, 0, 0], weight_ref.at[0, 0], count_ref, rows_ref, edge_ref, line_ref
    )
    add_column(column, line_ref, faces)


def transform_body(
    h_ref, k_ref, l_ref, head_ref, mid_ref, tail_ref, out_ref, grid_ref, shift_ref,
    table_ref, phase_y_ref, phase_x_ref, along_z_ref, half_ref, wave_ref, sems, *, totals,
):
    rows_x, rows_y, depth = grid_ref.shape
    copies = []
    start = 0
    for n, ref in enumerate((head_ref, mid_ref, tail_ref)):
        copies.append(pltpu.make_async_copy(ref, grid_ref.at[pl.ds(start, ref.shape[0])], sems.at[n]))
        copies[-1].start()
        start += ref.shape[0]
    place = (lax.axis_index("gx") * (rows_x - 7) - 3, lax.axis_index("gy") * (rows_y - 8) - 4)
    phase_tables(
        place, (h_ref, k_ref, l_ref), (*totals, depth), shift_ref, table_ref, phase_y_ref, phase_x_ref
    )
    for copy in copies:
        copy.wait()
    transforms(grid_ref, table_ref, phase_y_ref, phase_x_ref, along_z_ref, half_ref, wave_ref, out_ref)


FAR_AWAY = pl.BlockSpec(memory_space=pl.ANY)
NEARBY = pl.BlockSpec(memory_space=pltpu.VMEM)


def deposit(cell, frac, weight, count):
    _, columns, blocks_z, cap = weight.shape
    depth = 8 * blocks_z
    rows_y = 8 * columns + 8

    def turned(value):
        return jnp.swapaxes(value, -1, -2)

    f32 = jnp.float32
    faces = [(n, rows_y, depth) for n in (3, 8, 4)]
    atoms = pl.BlockSpec((3, 1, 1, cap, blocks_z), lambda j: (0, 0, j, 0, 0))
    return pl.pallas_call(
        deposit_body,
        grid=(columns,),
        in_specs=[
            pl.BlockSpec(count.shape, lambda j: (0, 0, 0)),
            atoms,
            atoms,
            pl.BlockSpec((1, 1, cap, blocks_z), lambda j: (0, j, 0, 0)),
        ],
        out_specs=[pl.BlockSpec(face, lambda j: (0, 0, 0)) for face in faces],
        out_shape=[jax.ShapeDtypeStruct(face, f32) for face in faces],
        scratch_shapes=[
            pltpu.VMEM((8, blocks_z // 2 // UNROLL, UNROLL, 2 * cap), f32),
            pltpu.VMEM((2 * (2 * cap // 128), 16, 128), f32),
            pltpu.VMEM((4, depth + 8, 64), f32),
        ],
        compiler_params=pltpu.CompilerParams(vmem_limit_bytes=62 << 20),
    )(count, turned(cell), turned(frac), turned(weight))


def transform(faces, miller_h, miller_k, miller_l, totals, pieces):
    _, rows_y, depth = faces[0].shape
    rows_x = sum(face.shape[0] for face in faces)
    wide = 16 * miller_h.shape[0]
    smem = pl.BlockSpec(memory_space=pltpu.SMEM)
    f32 = jnp.float32
    return pl.pallas_call(
        functools.partial(transform_body, totals=totals),
        in_specs=[smem] * 3 + [FAR_AWAY] * 3,
        out_specs=NEARBY,
        out_shape=jax.ShapeDtypeStruct((pieces, 16, 32 * wide // pieces), f32),
        scratch_shapes=[
            pltpu.VMEM((rows_x, rows_y, depth), f32),
            pltpu.VMEM((2, depth // FINE, wide), f32),
            pltpu.VMEM((2, depth, 2 * wide), jnp.bfloat16),
            pltpu.VMEM((rows_y, 32, wide), f32),
            pltpu.VMEM((rows_x, 32, wide), f32),
            pltpu.VMEM((rows_x, rows_y, 2 * wide), f32),
            pltpu.VMEM((rows_x, 32, wide), f32),
            pltpu.VMEM((512, wide), f32),
            pltpu.SemaphoreType.DMA((3,)),
        ],
        compiler_params=pltpu.CompilerParams(vmem_limit_bytes=62 << 20),
        cost_estimate=pl.CostEstimate(flops=5_000_000_000, bytes_accessed=8_000_000, transcendentals=0),
    )(miller_h, miller_k, miller_l, *faces)


def exchange(head, tail, axis):
    count = lax.axis_size(axis)
    before = lax.ppermute(tail, axis, [(i, (i + 1) % count) for i in range(count)])
    after = lax.ppermute(head, axis, [((i + 1) % count, i) for i in range(count)])
    return before, after


def added(inner, before, after, dim):
    length = inner.shape[dim]
    widths = [(0, 0)] * inner.ndim
    widths[dim] = (0, length - before.shape[dim])
    leading = jnp.pad(before, widths)
    widths[dim] = (length - after.shape[dim], 0)
    return inner + leading + jnp.pad(after, widths)


def shards(atom_cell, atom_frac, atom_weight, block_count, miller_h, miller_k, miller_l):
    blocks_x, blocks_y, blocks_z, _ = atom_weight.shape
    count_x, count_y = lax.axis_size("gx"), lax.axis_size("gy")
    width_x, width_y, depth = 8 * blocks_x, 8 * blocks_y, 8 * blocks_z
    total_x, total_y = width_x * count_x, width_y * count_y
    pieces = count_x * count_y
    head, mid, tail = deposit(atom_cell, atom_frac, atom_weight, block_count)
    before, after = exchange(head, tail, "gx")
    waves = transform((head, mid, tail), miller_h, miller_k, miller_l, (total_x, total_y), pieces)
    before, after, _ = lax.optimization_barrier((before, after, waves))
    received = lax.all_to_all(waves, ("gx", "gy"), 0, 0, tiled=False)
    rows = miller_h.shape[0] * 16 // pieces
    summed = jnp.sum(received, axis=0).reshape(16, rows, 2, 16)
    power = jnp.sum(summed * summed, axis=2) / float(total_x * total_y * depth)
    intensity = jnp.transpose(power, (1, 2, 0)).reshape(rows, 256)
    wide = added(mid, before, after, 0)
    before, after = exchange(wide[:, :4], wide[:, width_y + 4 :], "gy")
    density = added(wide[:, 4 : width_y + 4], before, after, 1)
    return (density, intensity)


def solution(mesh):
    in_specs = (
        P(None, "gx", "gy", None, None),
        P(None, "gx", "gy", None, None),
        P("gx", "gy", None, None),
        P("gx", "gy", None),
        P(),
        P(),
        P(),
    )
    out_specs = (P("gx", "gy", None), P(("gx", "gy"), None))
    return jax.shard_map(shards, mesh=mesh, in_specs=in_specs, out_specs=out_specs, check_vma=False)
```

```python
import functools
import math

import jax
import jax.numpy as jnp
from jax import lax
from jax.experimental import pallas as pl
from jax.experimental.pallas import tpu as pltpu
from jax.sharding import PartitionSpec as P

KERNEL_SIGMA = 0.9
NORMAL = 1.0 / (KERNEL_SIGMA * math.sqrt(2.0 * math.pi))
SCALE = math.sqrt(0.5 / math.log(2.0)) / KERNEL_SIGMA
LOG_NORMAL = math.log2(NORMAL)
FAR = -1.0e4
LANES_BY_LANES = (((1,), (1,)), ((), ()))
UNROLL = 32
FINE = 32


def turn(freqs, place, extent):
    product = freqs * place
    if extent & (extent - 1) == 0:
        product = product & (extent - 1)
    else:
        product = lax.rem(lax.rem(product, extent) + extent, extent)
    if extent & (extent - 1) or extent < 8:
        angle = product.astype(jnp.float32) * (2.0 * math.pi / extent)
        return jnp.cos(angle), jnp.sin(angle)
    quarters = (product + extent // 8) >> ((extent // 4).bit_length() - 1)
    angle = (product - quarters * (extent // 4)).astype(jnp.float32) * (2.0 * math.pi / extent)
    square = angle * angle
    cos = jnp.full_like(angle, -1.0 / math.factorial(10))
    for n in (8, 6, 4, 2, 0):
        cos = cos * square + (-1.0) ** (n // 2) / math.factorial(n)
    sin = jnp.full_like(angle, 1.0 / math.factorial(9))
    for n in (7, 5, 3, 1):
        sin = sin * square + (-1.0) ** (n // 2) / math.factorial(n)
    sin = sin * angle
    odd = (quarters & 1) == 1
    cos, sin = jnp.where(odd, sin, cos), jnp.where(odd, cos, sin)
    cos = jnp.where(((quarters + 1) & 2) == 2, -cos, cos)
    return cos, jnp.where((quarters & 2) == 2, -sin, sin)


def times(one, other):
    return (
        one[0] * other[0] - one[1] * other[1],
        one[0] * other[1] + one[1] * other[0],
    )


def split(value):
    head = value.astype(jnp.bfloat16)
    return head, (value - head.astype(jnp.float32)).astype(jnp.bfloat16)


def phase_tables(place, millers, extents, shift_ref, table_ref, phase_y_ref, phase_x_ref):
    h_ref, k_ref, l_ref = millers
    total_x, total_y, depth = extents
    windows = h_ref.shape[0]
    wide = 16 * windows

    def centres(ref, rows):
        window = lax.broadcasted_iota(jnp.int32, (rows, wide), 1) // 16
        found = jnp.zeros((rows, wide), jnp.int32)
        for w in range(windows):
            found = jnp.where(window == w, ref[w], found)
        return found - 8

    lane = lax.broadcasted_iota(jnp.int32, (FINE, wide), 1) % 16
    below = lax.broadcasted_iota(jnp.int32, (FINE, wide), 0)
    freq_l = centres(l_ref, FINE) + lane
    fine = turn(freq_l, below, depth)
    coarse = turn(freq_l, below * FINE, depth)
    shift_ref[0] = coarse[0]
    shift_ref[1] = coarse[1]
    for step in range(depth // FINE):
        now = times(fine, (shift_ref[0, step : step + 1], shift_ref[1, step : step + 1]))
        at = pl.ds(step * FINE, FINE)
        for side, value in ((0, now[0]), (1, -now[1])):
            head, rest = split(value)
            table_ref[0, at, side * wide : (side + 1) * wide] = head
            table_ref[1, at, side * wide : (side + 1) * wide] = rest
    row = lax.broadcasted_iota(jnp.int32, (16, wide), 0)
    for ref, out_ref, start, total in (
        (k_ref, phase_y_ref, place[1], total_y),
        (h_ref, phase_x_ref, place[0], total_x),
    ):
        freqs = centres(ref, 16) + row
        now = turn(freqs, start + 2 * total, total)
        step = turn(freqs, 1, total)
        for n in range(out_ref.shape[0]):
            out_ref[n, 0:16] = now[0]
            out_ref[n, 16:32] = now[1]
            now = times(now, step)


def transforms(faces, table_ref, phase_y_ref, phase_x_ref, along_z_ref, half_ref, wave_ref, out_ref):
    rows_x, rows_y, _ = along_z_ref.shape
    depth = faces[0].shape[2]
    wide = wave_ref.shape[1]

    def dot(a, b):
        return jnp.dot(a, b, preferred_element_type=jnp.float32)

    grid = jnp.concatenate([face[...].reshape(face.shape[0] * rows_y, depth) for face in faces], axis=0)
    value, rest = split(grid)
    found = dot(value, table_ref[0]) + (dot(value, table_ref[1]) + dot(rest, table_ref[0]))
    along_z_ref[...] = found.reshape(rows_x, rows_y, 2 * wide)
    group = 5 if rows_x % 5 == 0 else 1
    for x in range(0, rows_x, group):
        real = [jnp.zeros((16, wide), jnp.float32)] * group
        imag = [jnp.zeros((16, wide), jnp.float32)] * group
        for y in range(1, rows_y):
            cos = phase_y_ref[y, 0:16]
            sin = phase_y_ref[y, 16:32]
            for g in range(group):
                a = along_z_ref[x + g, y : y + 1, 0:wide]
                b = along_z_ref[x + g, y : y + 1, wide : 2 * wide]
                real[g] = real[g] + (a * cos + b * sin)
                imag[g] = imag[g] + (b * cos - a * sin)
        for g in range(group):
            half_ref[x + g, 0:16] = real[g]
            half_ref[x + g, 16:32] = imag[g]
    group = 4
    for h in range(0, 16, group):
        real = [jnp.zeros((16, wide), jnp.float32)] * group
        imag = [jnp.zeros((16, wide), jnp.float32)] * group
        for x in range(rows_x):
            a = half_ref[x, 0:16]
            b = half_ref[x, 16:32]
            for g in range(group):
                cos = phase_x_ref[x, h + g : h + g + 1]
                sin = phase_x_ref[x, 16 + h + g : 17 + h + g]
                real[g] = real[g] + (a * cos + b * sin)
                imag[g] = imag[g] + (b * cos - a * sin)
        for g in range(group):
            wave_ref[pl.ds(32 * (h + g), 16)] = real[g]
            wave_ref[pl.ds(32 * (h + g) + 16, 16)] = imag[g]
    turned = jnp.transpose(wave_ref[...])
    pieces, _, lanes = out_ref.shape
    per_window = pieces // (wide // 16)
    for piece in range(pieces):
        w, part = piece // per_window, piece % per_window
        out_ref[piece] = turned[16 * w : 16 * w + 16, part * lanes : (part + 1) * lanes]


def deposit_column(column, cell_ref, frac_ref, weight_ref, count_ref, rows_ref, edge_ref, line_ref):
    cap, blocks_z = weight_ref.shape
    depth = 8 * blocks_z
    half = blocks_z // 2
    two = 2 * cap

    def paired(value):
        value = jnp.transpose(value)
        return jnp.concatenate([value[:half], value[half:]], axis=1).reshape(half // UNROLL, UNROLL, two)

    line_ref[...] = jnp.zeros_like(line_ref)
    for d in range(3):
        cell = cell_ref[d].astype(jnp.float32)
        place = cell + frac_ref[d]
        if d == 0:
            upper = jnp.where(cell > 3.5, 1.0, 0.0)
            rows_ref[0] = paired((place - 3.5) * SCALE)
            rows_ref[1] = paired(upper)
            rows_ref[2] = paired(cell - 4.0 * upper)
        else:
            rows_ref[2 * d + 1] = paired(place * SCALE)
            rows_ref[2 * d + 2] = paired(cell)
    slots = lax.broadcasted_iota(jnp.int32, (cap, blocks_z), 0)
    rows_ref[7] = paired(jnp.where(slots < count_ref[0, pl.ds(column, 1), :], weight_ref[...], 0.0))
    row = lax.broadcasted_iota(jnp.int32, (8, 128), 0)
    row8 = row.astype(jnp.float32)
    low = (row8 - 4.0) * SCALE
    high = (row8 + 4.0) * SCALE
    row4 = (row % 4).astype(jnp.float32)
    second = row >= 4
    nodes = (4.0 * row4 - 6.0) * SCALE
    first = jnp.where(second, 1.0, 0.0)
    on_lower = jnp.where((row4 >= first) & (row4 <= first + 1.0), 0.0, FAR)
    on_upper = jnp.where((row4 >= first + 1.0) & (row4 <= first + 2.0), 0.0, FAR)
    slopes = (row4 - 1.5) * (2.0 * SCALE)
    sign = jnp.where(second, -1.0, 1.0)
    bound = jnp.where(second, 0.5 - row4, row4)
    part = cap % 128
    lanes = lax.broadcasted_iota(jnp.int32, (16, 128), 1)
    none = jnp.zeros((16, 128), jnp.bfloat16)

    def group(g, carry):
        for u in range(UNROLL):
            lefts = [[], []]
            rights = [[], []]
            for t in range(two // 128):

                def line(k):
                    return rows_ref[k, g, u : u + 1, 128 * t : 128 * t + 128]

                def taps(d):
                    inside = row8 > line(2 * d + 2)
                    away = jnp.where(inside, low, high) - line(2 * d + 1)
                    return inside, jnp.exp2(LOG_NORMAL - away * away)

                def halves(inside, value):
                    return jnp.concatenate([jnp.where(inside, value, 0.0), jnp.where(inside, 0.0, value)], axis=0)

                here = (u % 2) * (two // 128) + t
                place = line(0)
                away = place - nodes
                edge_ref[here, 0:8] = jnp.exp2(jnp.where(line(1) > 0.5, on_upper, on_lower) - away * away)
                edge_ref[here, 8:16] = jnp.exp2(jnp.where(bound > sign * line(2), slopes * place, FAR))
                inside, value = taps(1)
                taps_y = halves(inside, value)
                inside, value = taps(2)
                scaled = halves(inside, value * line(7))

                def rows(values, start, dead):
                    sides = []
                    for s in range(2):
                        sides.append(
                            jnp.concatenate(
                                [
                                    none
                                    if (s, n) in dead
                                    else (
                                        values * edge_ref[here, start + 4 * s + n : start + 4 * s + n + 1, :]
                                    ).astype(jnp.bfloat16)
                                    for n in range(4)
                                ],
                                axis=0,
                            )
                        )
                    return jnp.concatenate(sides, axis=1)

                right = rows(taps_y, 8, [(0, 0)])
                if part and t == cap // 128:
                    owned = [(0, jnp.where(lanes < part, scaled, 0.0)), (1, jnp.where(lanes < part, 0.0, scaled))]
                else:
                    owned = [(int(128 * t >= cap), scaled)]
                for side, values in owned:
                    lefts[side].append(rows(values, 0, [(0, 3), (1, 0)]))
                    rights[side].append(right)
            base = pl.multiple_of(8 * (g * UNROLL + u), 8)
            for s in range(2):
                found = lax.dot_general(
                    jnp.concatenate(lefts[s], axis=1),
                    jnp.concatenate(rights[s], axis=1),
                    LANES_BY_LANES,
                    preferred_element_type=jnp.float32,
                )
                for n in range(4):
                    line_ref[n, pl.ds(base + 8 * half * s, 16), :] += found[16 * n : 16 * n + 16]
        return carry

    lax.fori_loop(0, half // UNROLL, group, 0)


def add_column(column, line_ref, faces):
    depth = faces[0].shape[2]
    for n in range(4):
        line_ref[n, 4:8, :] += line_ref[n, depth + 4 : depth + 8, :]
        line_ref[n, depth : depth + 4, :] += line_ref[n, 0:4, :]
    at = pl.ds(pl.multiple_of(8 * column, 8), 16)
    for n in range(4):
        for c in range(depth // 128):
            turned = jnp.transpose(line_ref[n, 128 * c + 4 : 128 * c + 132, :])
            for k in range(4):
                near = k - 1.5
                factor = NORMAL * math.exp((-near * (4 * n - 6) - 0.5 * near * near) / KERNEL_SIGMA**2)
                face = faces[(n + 1) // 2]
                row = 4 * n + k - (1, 4, 12)[(n + 1) // 2]
                if row >= 0:
                    face[row, at, 128 * c : 128 * c + 128] += turned[16 * k : 16 * k + 16] * factor


def whole_body(
    h_ref, k_ref, l_ref, count_ref, cell_ref, frac_ref, weight_ref, head_ref, mid_ref, tail_ref, out_ref,
    rows_ref, edge_ref, line_ref, shift_ref, table_ref, phase_y_ref, phase_x_ref, along_z_ref, half_ref, wave_ref,
    *, totals,
):
    column = pl.program_id(0)
    faces = (head_ref, mid_ref, tail_ref)
    rows_x, rows_y, _ = along_z_ref.shape
    depth = mid_ref.shape[2]

    @pl.when(column == 0)
    def _():
        place = (lax.axis_index("gx") * (rows_x - 7) - 3, lax.axis_index("gy") * (rows_y - 8) - 4)
        phase_tables(
            place, (h_ref, k_ref, l_ref), (*totals, depth), shift_ref, table_ref, phase_y_ref, phase_x_ref
        )
        for face in faces:
            face[...] = jnp.zeros_like(face)

    deposit_column(
        column, cell_ref.at[:, 0, 0], frac_ref.at[:, 0, 0], weight_ref.at[0, 0], count_ref, rows_ref, edge_ref, line_ref
    )
    add_column(column, line_ref, faces)

    @pl.when(column == pl.num_programs(0) - 1)
    def _():
        transforms(faces, table_ref, phase_y_ref, phase_x_ref, along_z_ref, half_ref, wave_ref, out_ref)


def deposit_and_transform(cell, frac, weight, count, miller_h, miller_k, miller_l, totals, pieces):
    _, columns, blocks_z, cap = weight.shape
    depth = 8 * blocks_z
    rows_x, rows_y = 15, 8 * columns + 8
    wide = 16 * miller_h.shape[0]

    def turned(value):
        return jnp.swapaxes(value, -1, -2)

    f32 = jnp.float32
    outs = [(n, rows_y, depth) for n in (3, 8, 4)] + [(pieces, 16, 32 * wide // pieces)]
    atoms = pl.BlockSpec((3, 1, 1, cap, blocks_z), lambda j: (0, 0, j, 0, 0))
    smem = pl.BlockSpec(memory_space=pltpu.SMEM)
    return pl.pallas_call(
        functools.partial(whole_body, totals=totals),
        grid=(columns,),
        in_specs=[
            smem,
            smem,
            smem,
            pl.BlockSpec(count.shape, lambda j: (0, 0, 0)),
            atoms,
            atoms,
            pl.BlockSpec((1, 1, cap, blocks_z), lambda j: (0, j, 0, 0)),
        ],
        out_specs=[pl.BlockSpec(out, lambda j: (0, 0, 0)) for out in outs],
        out_shape=[jax.ShapeDtypeStruct(out, f32) for out in outs],
        scratch_shapes=[
            pltpu.VMEM((8, blocks_z // 2 // UNROLL, UNROLL, 2 * cap), f32),
            pltpu.VMEM((2 * (2 * cap // 128), 16, 128), f32),
            pltpu.VMEM((4, depth + 8, 64), f32),
            pltpu.VMEM((2, depth // FINE, wide), f32),
            pltpu.VMEM((2, depth, 2 * wide), jnp.bfloat16),
            pltpu.VMEM((rows_y, 32, wide), f32),
            pltpu.VMEM((rows_x, 32, wide), f32),
            pltpu.VMEM((rows_x, rows_y, 2 * wide), f32),
            pltpu.VMEM((rows_x, 32, wide), f32),
            pltpu.VMEM((512, wide), f32),
        ],
        compiler_params=pltpu.CompilerParams(vmem_limit_bytes=62 << 20),
    )(miller_h, miller_k, miller_l, count, turned(cell), turned(frac), turned(weight))


def exchange(head, tail, axis):
    count = lax.axis_size(axis)
    before = lax.ppermute(tail, axis, [(i, (i + 1) % count) for i in range(count)])
    after = lax.ppermute(head, axis, [((i + 1) % count, i) for i in range(count)])
    return before, after


def added(inner, before, after, dim):
    length = inner.shape[dim]
    widths = [(0, 0)] * inner.ndim
    widths[dim] = (0, length - before.shape[dim])
    leading = jnp.pad(before, widths)
    widths[dim] = (length - after.shape[dim], 0)
    return inner + leading + jnp.pad(after, widths)


def shards(atom_cell, atom_frac, atom_weight, block_count, miller_h, miller_k, miller_l):
    blocks_x, blocks_y, blocks_z, _ = atom_weight.shape
    count_x, count_y = lax.axis_size("gx"), lax.axis_size("gy")
    width_x, width_y, depth = 8 * blocks_x, 8 * blocks_y, 8 * blocks_z
    total_x, total_y = width_x * count_x, width_y * count_y
    pieces = count_x * count_y
    head, mid, tail, waves = deposit_and_transform(
        atom_cell, atom_frac, atom_weight, block_count, miller_h, miller_k, miller_l, (total_x, total_y), pieces
    )
    received = lax.all_to_all(waves, ("gx", "gy"), 0, 0, tiled=False)
    before, after = exchange(head, tail, "gx")
    rows = miller_h.shape[0] * 16 // pieces
    summed = jnp.sum(received, axis=0).reshape(16, rows, 2, 16)
    power = jnp.sum(summed * summed, axis=2) / float(total_x * total_y * depth)
    intensity = jnp.transpose(power, (1, 2, 0)).reshape(rows, 256)
    wide = added(mid, before, after, 0)
    before, after = exchange(wide[:, :4], wide[:, width_y + 4 :], "gy")
    density = added(wide[:, 4 : width_y + 4], before, after, 1)
    return (density, intensity)


def solution(mesh):
    in_specs = (
        P(None, "gx", "gy", None, None),
        P(None, "gx", "gy", None, None),
        P("gx", "gy", None, None),
        P("gx", "gy", None),
        P(),
        P(),
        P(),
    )
    out_specs = (P("gx", "gy", None), P(("gx", "gy"), None))
    return jax.shard_map(shards, mesh=mesh, in_specs=in_specs, out_specs=out_specs, check_vma=False)
```
